1024 devices in a mesh: layer: 4 (over x_lo, core), row: 8 (over x_hi, y), col: 32 (over z).
Axes of the slice: x: 4 (x_hi: 2, x_lo: 2; x = x_hi * 2 + x_lo), y: 4, z: 32, core: 2. Of those that a mesh axis runs over, the one named last changes fastest.
Arguments:
- left_blocks: float32 [4, 8, 32, 2, 256, 256], P('layer', 'row', 'col'), may hold values from -6 to 6
- right_blocks: float32 [4, 8, 32, 2, 256, 256], P('layer', 'row', 'col'), may hold values from -0.1875 to 0.1875
- left_index: int32 [4, 8, 32, 2, 12], P('layer', 'row', 'col'), may hold values from 0 to 1
- right_index: int32 [4, 8, 32, 2, 12], P('layer', 'row', 'col'), may hold values from 0 to 1
- target_index: int32 [4, 8, 32, 2, 12], P('layer', 'row', 'col'), may hold values from 0 to 3
- live_counts: int32 [4, 8, 32, 2], P('layer', 'row', 'col'), may hold values from 3 to 12, as said below
- keep_mask: int32 [8, 32, 4], P('row', 'col', 'layer'), may hold values 0 or 1
Outputs:
- product_blocks: float32 [8, 32, 4, 256, 256], P('row', 'col', 'layer')
The draws below stay inside these ranges and needn't reach their ends.
Inputs may be any that keep to these rules, and one draw needn't show every extreme that they name: `live_counts`: every count is at most 12, and some device and step has exactly 12 live slots.
All inputs are finite; a program needn't handle non-finite values. No bound on the sum of `keep_mask` on one device may be relied on, other than what follows from the above.
Results may differ from the reference program's by a relative error of at most 0.0003.
Values sent between devices are 32-bit elements; how exact they have to be, the bound alone decides.
No kernel may reach another device: no remote copies, remote signals or barrier semaphores. Data moves between devices by JAX's collectives and lax.ppermute only.
A program may use at most 32 MiB of HBM per device.

```python
import jax
import jax.numpy as jnp
from jax import lax

BLOCK = 256
SLOTS = 2
PRODS = 12
CBLOCKS = 4
STEPS = 2
N_LAYER = 4
N_ROW = 8
N_COL = 32


def draw_live_counts(key, part):
    key = jax.random.fold_in(key, 7)
    values = jax.random.randint(key, (N_LAYER, N_ROW, N_COL, STEPS), max(PRODS // 4, 1), PRODS + 1)
    return values.at[0, 0, 0, 0].set(PRODS).astype(jnp.int32)


def set_ends(entries, key, low, top_value):
    spot = [jax.random.randint(jax.random.fold_in(key, axis), (), 0, length) for axis, length in enumerate(entries.shape)]
    longest = entries.shape.index(max(entries.shape))
    neighbour = spot[:longest] + [(spot[longest] + 1) % entries.shape[longest]] + spot[longest + 1:]
    return entries.at[tuple(spot)].set(low).at[tuple(neighbour)].set(top_value)


def level_of(stream_key, shape, shards, smallest, largest):
    def one(axis_at, blocks):
        heights = jax.random.uniform(jax.random.fold_in(jax.random.fold_in(stream_key, 6), axis_at), (blocks,), jnp.float32, smallest / len(shards), largest / len(shards))
        return jnp.repeat(jnp.exp(heights), shape[axis_at] // blocks).reshape((-1,) + (1,) * (len(shape) - axis_at - 1))

    gain = one(*shards[0])
    for cut in shards[1:]:
        gain = gain * one(*cut)
    return gain


def centred(key, shape, deviation, most, split=(), held_as=jnp.bfloat16):
    gain = level_of(key, shape, split, -0.22, 0.18) if split else 1.0
    array = jax.random.normal(key, shape, jnp.float32) * deviation * gain
    return jnp.minimum(jnp.maximum(array, -most), most).astype(held_as)


def setup_inputs(seed: int = 0) -> dict:
    key_list = jax.random.split(jax.random.key(seed), 8)
    return {
        "left_blocks": centred(key_list[0], (N_LAYER, N_ROW, N_COL, SLOTS, BLOCK, BLOCK), 1.0, 6.0, ((0, 4), (1, 8), (2, 32)), jnp.float32),
        "right_blocks": centred(key_list[1], (N_LAYER, N_ROW, N_COL, SLOTS, BLOCK, BLOCK), (4 * BLOCK) ** -0.5, 0.1875, ((0, 4), (1, 8), (2, 32)), jnp.float32),
        "left_index": set_ends(jax.random.randint(key_list[2], (N_LAYER, N_ROW, N_COL, STEPS, PRODS), 0, SLOTS), jax.random.fold_in(key_list[2], 1), 0, SLOTS - 1).astype(jnp.int32),
        "right_index": set_ends(jax.random.randint(key_list[3], (N_LAYER, N_ROW, N_COL, STEPS, PRODS), 0, SLOTS), jax.random.fold_in(key_list[3], 1), 0, SLOTS - 1).astype(jnp.int32),
        "target_index": set_ends(jax.random.randint(key_list[4], (N_LAYER, N_ROW, N_COL, STEPS, PRODS), 0, CBLOCKS), jax.random.fold_in(key_list[4], 1), 0, CBLOCKS - 1).astype(jnp.int32),
        "live_counts": draw_live_counts(jax.random.fold_in(key_list[7], 71), 0),
        "keep_mask": set_ends((jax.random.randint(key_list[6], (N_ROW, N_COL, CBLOCKS), 0, 4) < 3).astype(jnp.int32), jax.random.fold_in(key_list[6], 1), 0, 1),
    }


def one_layer(total, pieces):
    left_layer, right_layer, left_sel, right_sel, target_sel, count_sel = pieces
    slot_ids = jnp.arange(PRODS, dtype=jnp.int32)
    block_ids = jnp.arange(CBLOCKS, dtype=jnp.int32)
    for step in range(STEPS):
        left_tile = jnp.roll(left_layer, step, axis=1)
        right_tile = jnp.roll(right_layer, step, axis=0)
        left_pick = jnp.take_along_axis(left_tile, left_sel[:, :, step][..., None, None], axis=2)
        right_pick = jnp.take_along_axis(right_tile, right_sel[:, :, step][..., None, None], axis=2)
        terms = jnp.einsum("rcpij,rcpjk->rcpik", left_pick, right_pick, precision=lax.Precision.HIGHEST)
        live = (slot_ids[None, None, :] < count_sel[:, :, step][..., None]).astype(jnp.float32)
        onehot = (target_sel[:, :, step][..., None] == block_ids).astype(jnp.float32) * live[..., None]
        total = total + jnp.einsum("rcpq,rcpik->rcqik", onehot, terms, precision=lax.Precision.HIGHEST)
    return total, None


def reference(left_blocks, right_blocks, left_index, right_index, target_index, live_counts, keep_mask):
    start = jnp.zeros((N_ROW, N_COL, CBLOCKS, BLOCK, BLOCK), jnp.float32)
    summed, unused = lax.scan(one_layer, start, (left_blocks, right_blocks, left_index, right_index, target_index, live_counts))
    return summed * keep_mask.astype(jnp.float32)[..., None, None]
```

```python
import functools

import jax
import jax.numpy as jnp
from jax import lax
from jax.experimental import pallas as pl
from jax.experimental.pallas import tpu as pltpu
from jax.sharding import PartitionSpec as P

VMEM = pltpu.VMEM
SMEM = pltpu.SMEM


def count_pairs(step, layer, li, ri, ti, counts, table, where):
    for entry in range(16):
        table[where, entry] = 0.0
    live = counts[0, 0, 0, step]
    for p in range(li.shape[4]):
        spot = (ti[0, 0, 0, step, p] ^ layer) * 4 + li[0, 0, 0, step, p] * 2 + ri[0, 0, 0, step, p]
        table[where, spot] = table[where, spot] + jnp.where(p < live, 1.0, 0.0)


def halves(value):
    high = value.astype(jnp.bfloat16)
    return high, (value - high.astype(jnp.float32)).astype(jnp.bfloat16)


def pair_products(left, right):
    slots, rows, depth = left.shape
    high, low = halves(left[...].reshape(slots * rows, depth))
    found = []
    for slot in range(right.shape[0]):
        right_high, right_low = halves(right[slot])
        dot = functools.partial(jnp.dot, preferred_element_type=jnp.float32)
        found.append(dot(high, right_high) + (dot(high, right_low) + dot(low, right_high)))
    return found


def combine(found, table, where, j, rows):
    total = None
    for l in range(2):
        for r in range(2):
            term = found[r][l * rows : (l + 1) * rows] * table[where, j * 4 + l * 2 + r]
            total = term if total is None else total + term
    return total


def first_kernel(li, ri, ti, counts, left, right, part, table_out, table):
    layer = lax.axis_index("layer")
    count_pairs(0, layer, li, ri, ti, counts, table, 0)
    count_pairs(1, layer, li, ri, ti, counts, table_out, 0)
    found = pair_products(left, right)
    for j in range(4):
        part[j] = combine(found, table, 0, j, left.shape[1])


def second_kernel(table, left, right, part, *outs):
    found = pair_products(left, right)
    for j in (2, 3, 1, 0):
        outs[j][...] = part[j] + combine(found, table, 0, j, left.shape[1])


def permute(value, axis, to):
    n = lax.axis_size(axis)
    return lax.ppermute(value, axis, [(i, to(i, n)) for i in range(n)])


def local(left_blocks, right_blocks, left_index, right_index, target_index, live_counts, keep_mask):
    left = left_blocks[0, 0, 0]
    right = right_blocks[0, 0, 0]
    rows = left.shape[1]
    right_next = permute(right, "row", lambda i, n: (i + 1) % n)
    left_next = permute(left, "col", lambda i, n: (i + 1) % n)
    block = jax.ShapeDtypeStruct((rows, rows), jnp.float32)
    vmem = pl.BlockSpec(memory_space=VMEM)
    smem = pl.BlockSpec(memory_space=SMEM)
    part, table = pl.pallas_call(
        first_kernel,
        out_shape=(jax.ShapeDtypeStruct((4, rows, rows), jnp.float32), jax.ShapeDtypeStruct((1, 16), jnp.float32)),
        in_specs=[smem] * 4 + [vmem] * 2,
        out_specs=(vmem, smem),
        scratch_shapes=[pltpu.SMEM((1, 16), jnp.float32)],
        compiler_params=pltpu.CompilerParams(vmem_limit_bytes=24 << 20),
        cost_estimate=pl.CostEstimate(flops=6 << 26, bytes_accessed=2 << 20, transcendentals=0),
        name="first_step",
    )(left_index, right_index, target_index, live_counts, left, right)
    own, core, chip, far = pl.pallas_call(
        second_kernel,
        out_shape=(block,) * 4,
        in_specs=[smem] + [vmem] * 3,
        out_specs=(vmem,) * 4,
        compiler_params=pltpu.CompilerParams(vmem_limit_bytes=24 << 20),
        cost_estimate=pl.CostEstimate(flops=6 << 26, bytes_accessed=3 << 20, transcendentals=0),
        name="second_step",
    )(table, left_next, right_next, part)
    chip = permute(chip, "layer", lambda i, n: i ^ 2)
    far = permute(far, "layer", lambda i, n: i ^ 3)
    core = permute(core, "layer", lambda i, n: i ^ 1)
    summed = (own + core) + (chip + far)
    result = summed * keep_mask[0, 0].astype(jnp.float32)[:, None, None]
    return result[None, None]


def solution(mesh):
    return jax.shard_map(
        local,
        mesh=mesh,
        in_specs=(
            P("layer", "row", "col", None, None, None),
            P("layer", "row", "col", None, None, None),
            P("layer", "row", "col", None, None),
            P("layer", "row", "col", None, None),
            P("layer", "row", "col", None, None),
            P("layer", "row", "col", None),
            P("row", "col", "layer"),
        ),
        out_specs=P("row", "col", "layer", None, None),
        check_vma=False,
    )
```

```python
import functools

import jax
import jax.numpy as jnp
from jax import lax
from jax.experimental import pallas as pl
from jax.experimental.pallas import tpu as pltpu
from jax.sharding import PartitionSpec as P

VMEM = pltpu.VMEM
SMEM = pltpu.SMEM
PARAMS = pltpu.CompilerParams(vmem_limit_bytes=24 << 20)
dot = functools.partial(jnp.dot, preferred_element_type=jnp.float32)


def count_pairs(step, layer, li, ri, ti, counts, table):
    for entry in range(16):
        table[0, entry] = 0.0
    live = counts[0, 0, 0, step]
    for p in range(li.shape[4]):
        spot = (ti[0, 0, 0, step, p] ^ layer) * 4 + li[0, 0, 0, step, p] * 2 + ri[0, 0, 0, step, p]
        table[0, spot] = table[0, spot] + jnp.where(p < live, 1.0, 0.0)


def halves(value):
    high = value.astype(jnp.bfloat16)
    return high, (value - high.astype(jnp.float32)).astype(jnp.bfloat16)


def pair_products(left, right_high, right_low, slots):
    count, rows, depth = left.shape
    high, low = halves(left.reshape(count * rows, depth))
    found = []
    for slot in slots:
        both = dot(high, right_high[slot]) + (dot(high, right_low[slot]) + dot(low, right_high[slot]))
        found.append([both[l * rows : (l + 1) * rows] for l in range(count)])
    return found


def combine(found, weight, j, total=None):
    for l in range(2):
        for r in range(2):
            term = found[r][l] * weight(j * 4 + l * 2 + r)
            total = term if total is None else total + term
    return total


def first_kernel(li, ri, ti, counts, left, right, keep, send, table, later):
    layer = lax.axis_index("layer")
    core = layer & 1
    count_pairs(0, layer, li, ri, ti, counts, table)
    count_pairs(1, layer, li, ri, ti, counts, later)
    half = left.shape[1] // 2
    width = send.shape[1]
    parts = [halves(right[slot]) for slot in range(2)]
    highs, lows = [part[0] for part in parts], [part[1] for part in parts]
    for out, side, flip in ((keep, core, 0), (send, 1 - core, 1)):
        begin = pl.multiple_of(side * half, half)
        found = pair_products(left[:, pl.ds(begin, half)], highs, lows, (0, 1))
        for j in range(4):
            spot = j ^ flip
            out[spot * half : (spot + 1) * half, :] = combine(found, lambda k: table[0, k], j)
            for k in range(4):
                row = 4 * half + spot * 4 + k
                out[row : row + 1, :] = jnp.full((1, width), later[0, j * 4 + k], jnp.float32)


def ready_kernel(right_own, right_mate, keep, heard, right_high, right_low, base, weights):
    for slot in range(4):
        right = (right_own if slot < 2 else right_mate)[slot % 2]
        right_high[slot], right_low[slot] = halves(right)
    size = base.shape[0]
    base[...] = keep[:size, :] + heard[:size, :]
    weights[:16] = keep[size:, :]
    weights[16:] = heard[size:, :]


def second_kernel(left_own, left_mate, right_high, right_low, base, weights, *outs):
    half = left_own.shape[1]
    own = pair_products(left_own[...], right_high, right_low, (0, 1))
    mate = pair_products(left_mate[...], right_high, right_low, (2, 3))
    for j in (2, 3, 1, 0):
        total = combine(own, lambda k: weights[k : k + 1, :], j, base[j * half : (j + 1) * half, :])
        outs[j][...] = combine(mate, lambda k: weights[16 + k : 17 + k, :], j, total)


def last_kernel(mask, chip, far, core, own, out, held, sems):
    side = lax.axis_index("layer") & 1
    scale = mask[0, 0, 0].astype(jnp.float32)
    half = own.shape[0]
    copies = []
    for other, (a, b) in enumerate(((own, chip), (core, far))):
        held[other * half : (other + 1) * half] = (a[...] + b[...]) * scale
        begin = pl.multiple_of((side if other == 0 else 1 - side) * half, half)
        copies.append(pltpu.make_async_copy(held.at[pl.ds(other * half, half)], out.at[pl.ds(begin, half)], sems.at[other]))
        copies[-1].start()
    for copy in copies:
        copy.wait()


def permute(value, to):
    names = ("layer", "row", "col")
    sizes = [lax.axis_size(name) for name in names]
    pairs = []
    for l in range(sizes[0]):
        for r in range(sizes[1]):
            for c in range(sizes[2]):
                ln, rn, cn = to(l, r, c)
                pairs.append(((l * sizes[1] + r) * sizes[2] + c, (ln * sizes[1] + rn % sizes[1]) * sizes[2] + cn % sizes[2]))
    return lax.ppermute(value, names, pairs)


def local(left_blocks, right_blocks, left_index, right_index, target_index, live_counts, keep_mask):
    left = left_blocks[0, 0, 0]
    right = right_blocks[0, 0, 0]
    slots, rows, cols = left.shape
    half = rows // 2
    f32 = jnp.float32
    core = lax.axis_index("layer") & 1
    vmem = pl.BlockSpec(memory_space=VMEM)
    smem = pl.BlockSpec(memory_space=SMEM)
    anywhere = pl.BlockSpec(memory_space=pl.ANY)

    def piece(side):
        return lax.dynamic_slice_in_dim(left, side * half, half, 1, allow_negative_indices=False)

    pieces = [piece(core), piece(1 - core)]
    left, right, *pieces = lax.optimization_barrier((left, right, *pieces))
    left_own = permute(pieces[0], lambda l, r, c: (l, r, c + 1))
    left_mate = permute(pieces[1], lambda l, r, c: (l ^ 1, r, c + 1))

    def middle(left, right):
        right_own = permute(right, lambda l, r, c: (l, r + 1, c))
        right_mate = permute(right_own, lambda l, r, c: (l ^ 1, r, c))
        keep, send = pl.pallas_call(
            first_kernel,
            out_shape=(jax.ShapeDtypeStruct((4 * half + 16, cols), f32),) * 2,
            in_specs=[smem] * 4 + [vmem] * 2,
            out_specs=(vmem, vmem),
            scratch_shapes=[pltpu.SMEM((1, 16), f32)] * 2,
            compiler_params=PARAMS,
            cost_estimate=pl.CostEstimate(flops=6 << 26, bytes_accessed=2 << 20, transcendentals=0),
            name="first_step",
        )(left_index, right_index, target_index, live_counts, left, right)
        heard = permute(send, lambda l, r, c: (l ^ 1, r, c))
        return pl.pallas_call(
            ready_kernel,
            out_shape=(
                jax.ShapeDtypeStruct((4, rows, cols), jnp.bfloat16),
                jax.ShapeDtypeStruct((4, rows, cols), jnp.bfloat16),
                jax.ShapeDtypeStruct((4 * half, cols), f32),
                jax.ShapeDtypeStruct((32, cols), f32),
            ),
            in_specs=[vmem] * 4,
            out_specs=(vmem,) * 4,
            compiler_params=PARAMS,
            cost_estimate=pl.CostEstimate(flops=1 << 20, bytes_accessed=4 << 20, transcendentals=0),
            name="ready",
        )(right_own, right_mate, keep, heard)

    shapes = jax.eval_shape(middle, left, right)
    within = live_counts[0, 0, 0, 0] <= left_index.shape[4]
    ready = lax.cond(within, middle, lambda *args: tuple(jnp.zeros(s.shape, s.dtype) for s in shapes), left, right)
    own, core_out, chip_out, far_out = pl.pallas_call(
        second_kernel,
        out_shape=(jax.ShapeDtypeStruct((half, cols), f32),) * 4,
        in_specs=[vmem] * 6,
        out_specs=(vmem,) * 4,
        compiler_params=PARAMS,
        cost_estimate=pl.CostEstimate(flops=6 << 26, bytes_accessed=3 << 20, transcendentals=0),
        name="second_step",
    )(left_own, left_mate, *ready)
    chip_in = permute(chip_out, lambda l, r, c: (l ^ 2, r, c))
    far_in = permute(far_out, lambda l, r, c: (l ^ 3, r, c))
    core_in = permute(core_out, lambda l, r, c: (l ^ 1, r, c))
    result = pl.pallas_call(
        last_kernel,
        out_shape=jax.ShapeDtypeStruct((rows, cols), f32),
        in_specs=[smem] + [vmem] * 4,
        out_specs=anywhere,
        scratch_shapes=[pltpu.VMEM((rows, cols), f32), pltpu.SemaphoreType.DMA((2,))],
        compiler_params=PARAMS,
        cost_estimate=pl.CostEstimate(flops=1 << 18, bytes_accessed=1 << 20, transcendentals=0),
        name="last_sum",
    )(keep_mask, chip_in, far_in, core_in, own)
    return result[None, None, None]


def solution(mesh):
    return jax.shard_map(
        local,
        mesh=mesh,
        in_specs=(
            P("layer", "row", "col", None, None, None),
            P("layer", "row", "col", None, None, None),
            P("layer", "row", "col", None, None),
            P("layer", "row", "col", None, None),
            P("layer", "row", "col", None, None),
            P("layer", "row", "col", None),
            P("row", "col", "layer"),
        ),
        out_specs=P("row", "col", "layer", None, None),
        check_vma=False,
    )
```

```python
import functools

import jax
import jax.numpy as jnp
from jax import lax
from jax.experimental import pallas as pl
from jax.experimental.pallas import tpu as pltpu
from jax.sharding import PartitionSpec as P

VMEM = pltpu.VMEM
SMEM = pltpu.SMEM
PARAMS = pltpu.CompilerParams(vmem_limit_bytes=24 << 20)
dot = functools.partial(jnp.dot, preferred_element_type=jnp.float32)


def count_pairs(step, layer, li, ri, ti, counts, table):
    for entry in range(16):
        table[0, entry] = 0.0
    live = counts[0, 0, 0, step]
    for p in range(li.shape[4]):
        spot = (ti[0, 0, 0, step, p] ^ layer) * 4 + li[0, 0, 0, step, p] * 2 + ri[0, 0, 0, step, p]
        table[0, spot] = table[0, spot] + jnp.where(p < live, 1.0, 0.0)


def halves(value):
    high = value.astype(jnp.bfloat16)
    return high, (value - high.astype(jnp.float32)).astype(jnp.bfloat16)


def pair_products(left, right_high, right_low, slots):
    count, rows, depth = left.shape
    high, low = halves(left.reshape(count * rows, depth))
    found = []
    for slot in slots:
        both = dot(high, right_high[slot]) + (dot(high, right_low[slot]) + dot(low, right_high[slot]))
        found.append([both[l * rows : (l + 1) * rows] for l in range(count)])
    return found


def combine(found, weight, j, total=None):
    for l in range(2):
        for r in range(2):
            term = found[r][l] * weight(j * 4 + l * 2 + r)
            total = term if total is None else total + term
    return total


def first_kernel(li, ri, ti, counts, left, right, keep, send, table, later):
    layer = lax.axis_index("layer")
    core = layer & 1
    count_pairs(0, layer, li, ri, ti, counts, table)
    count_pairs(1, layer, li, ri, ti, counts, later)
    half = left.shape[1] // 2
    width = send.shape[1]
    parts = [halves(right[slot]) for slot in range(2)]
    highs, lows = [part[0] for part in parts], [part[1] for part in parts]
    for out, side, flip in ((keep, core, 0), (send, 1 - core, 1)):
        begin = pl.multiple_of(side * half, half)
        found = pair_products(left[:, pl.ds(begin, half)], highs, lows, (0, 1))
        for j in range(4):
            spot = j ^ flip
            out[spot * half : (spot + 1) * half, :] = combine(found, lambda k: table[0, k], j)
            for k in range(4):
                row = 4 * half + spot * 4 + k
                out[row : row + 1, :] = jnp.full((1, width), later[0, j * 4 + k], jnp.float32)


def join_kernel(keep, heard, base, weights):
    size = base.shape[0]
    base[...] = keep[:size, :] + heard[:size, :]
    weights[:16] = keep[size:, :]
    weights[16:] = heard[size:, :]


def ready_kernel(right_own, right_mate, right_high, right_low):
    for slot in range(4):
        right = (right_own if slot < 2 else right_mate)[slot % 2]
        right_high[slot], right_low[slot] = halves(right)


def second_kernel(left_own, left_mate, right_high, right_low, base, weights, *outs):
    half = left_own.shape[1]
    own = pair_products(left_own[...], right_high, right_low, (0, 1))
    mate = pair_products(left_mate[...], right_high, right_low, (2, 3))
    for j in (2, 3, 1, 0):
        total = combine(own, lambda k: weights[k : k + 1, :], j, base[j * half : (j + 1) * half, :])
        outs[j][...] = combine(mate, lambda k: weights[16 + k : 17 + k, :], j, total)


def last_kernel(mask, chip, far, core, own, out, held, sems):
    side = lax.axis_index("layer") & 1
    scale = mask[0, 0, 0].astype(jnp.float32)
    half = own.shape[0]
    copies = []
    for other, (a, b) in enumerate(((own, chip), (core, far))):
        held[other * half : (other + 1) * half] = (a[...] + b[...]) * scale
        begin = pl.multiple_of((side if other == 0 else 1 - side) * half, half)
        copies.append(pltpu.make_async_copy(held.at[pl.ds(other * half, half)], out.at[pl.ds(begin, half)], sems.at[other]))
        copies[-1].start()
    for copy in copies:
        copy.wait()


def permute(value, to):
    names = ("layer", "row", "col")
    sizes = [lax.axis_size(name) for name in names]
    pairs = []
    for l in range(sizes[0]):
        for r in range(sizes[1]):
            for c in range(sizes[2]):
                ln, rn, cn = to(l, r, c)
                pairs.append(((l * sizes[1] + r) * sizes[2] + c, (ln * sizes[1] + rn % sizes[1]) * sizes[2] + cn % sizes[2]))
    return lax.ppermute(value, names, pairs)


def local(left_blocks, right_blocks, left_index, right_index, target_index, live_counts, keep_mask):
    left = left_blocks[0, 0, 0]
    right = right_blocks[0, 0, 0]
    slots, rows, cols = left.shape
    half = rows // 2
    f32 = jnp.float32
    core = lax.axis_index("layer") & 1
    vmem = pl.BlockSpec(memory_space=VMEM)
    smem = pl.BlockSpec(memory_space=SMEM)
    anywhere = pl.BlockSpec(memory_space=pl.ANY)

    def piece(side):
        return lax.dynamic_slice_in_dim(left, side * half, half, 1, allow_negative_indices=False)

    right_own = permute(right, lambda l, r, c: (l, r + 1, c))
    left_own = permute(piece(core), lambda l, r, c: (l, r, c + 1))
    left_mate = permute(piece(1 - core), lambda l, r, c: (l ^ 1, r, c + 1))
    def beside(left, right):
        keep, send = pl.pallas_call(
            first_kernel,
            out_shape=(jax.ShapeDtypeStruct((4 * half + 16, cols), f32),) * 2,
            in_specs=[smem] * 4 + [vmem] * 2,
            out_specs=(vmem, vmem),
            scratch_shapes=[pltpu.SMEM((1, 16), f32)] * 2,
            compiler_params=PARAMS,
            cost_estimate=pl.CostEstimate(flops=6 << 26, bytes_accessed=2 << 20, transcendentals=0),
            name="first_step",
        )(left_index, right_index, target_index, live_counts, left, right)
        heard = permute(send, lambda l, r, c: (l ^ 1, r, c))
        return pl.pallas_call(
            join_kernel,
            out_shape=(jax.ShapeDtypeStruct((4 * half, cols), f32), jax.ShapeDtypeStruct((32, cols), f32)),
            in_specs=[vmem] * 2,
            out_specs=(vmem,) * 2,
            compiler_params=PARAMS,
            cost_estimate=pl.CostEstimate(flops=1 << 17, bytes_accessed=3 << 19, transcendentals=0),
            name="join",
        )(keep, heard)

    def middle(right_own):
        right_mate = permute(right_own, lambda l, r, c: (l ^ 1, r, c))
        return pl.pallas_call(
            ready_kernel,
            out_shape=(jax.ShapeDtypeStruct((4, rows, cols), jnp.bfloat16),) * 2,
            in_specs=[vmem] * 2,
            out_specs=(vmem,) * 2,
            compiler_params=PARAMS,
            cost_estimate=pl.CostEstimate(flops=1 << 20, bytes_accessed=2 << 20, transcendentals=0),
            name="ready",
        )(right_own, right_mate)

    within = live_counts[0, 0, 0, 0] <= left_index.shape[4]

    def guarded(branch, *args):
        shapes = jax.eval_shape(branch, *args)
        return lax.cond(within, branch, lambda *_: tuple(jnp.zeros(s.shape, s.dtype) for s in shapes), *args)

    base, weights = guarded(beside, left, right)
    right_high, right_low = guarded(middle, right_own)
    own, core_out, chip_out, far_out = pl.pallas_call(
        second_kernel,
        out_shape=(jax.ShapeDtypeStruct((half, cols), f32),) * 4,
        in_specs=[vmem] * 6,
        out_specs=(vmem,) * 4,
        compiler_params=PARAMS,
        cost_estimate=pl.CostEstimate(flops=6 << 26, bytes_accessed=3 << 20, transcendentals=0),
        name="second_step",
    )(left_own, left_mate, right_high, right_low, base, weights)
    chip_in = permute(chip_out, lambda l, r, c: (l ^ 2, r, c))
    far_in = permute(far_out, lambda l, r, c: (l ^ 3, r, c))
    core_in = permute(core_out, lambda l, r, c: (l ^ 1, r, c))
    result = pl.pallas_call(
        last_kernel,
        out_shape=jax.ShapeDtypeStruct((rows, cols), f32),
        in_specs=[smem] + [vmem] * 4,
        out_specs=anywhere,
        scratch_shapes=[pltpu.VMEM((rows, cols), f32), pltpu.SemaphoreType.DMA((2,))],
        compiler_params=PARAMS,
        cost_estimate=pl.CostEstimate(flops=1 << 18, bytes_accessed=1 << 20, transcendentals=0),
        name="last_sum",
    )(keep_mask, chip_in, far_in, core_in, own)
    return result[None, None, None]


def solution(mesh):
    return jax.shard_map(
        local,
        mesh=mesh,
        in_specs=(
            P("layer", "row", "col", None, None, None),
            P("layer", "row", "col", None, None, None),
            P("layer", "row", "col", None, None),
            P("layer", "row", "col", None, None),
            P("layer", "row", "col", None, None),
            P("layer", "row", "col", None),
            P("row", "col", "layer"),
        ),
        out_specs=P("row", "col", "layer", None, None),
        check_vma=False,
    )
```

```python
import functools

import jax
import jax.numpy as jnp
from jax import lax
from jax.experimental import pallas as pl
from jax.experimental.pallas import tpu as pltpu
from jax.sharding import PartitionSpec as P

VMEM = pltpu.VMEM
SMEM = pltpu.SMEM
PARAMS = pltpu.CompilerParams(vmem_limit_bytes=24 << 20)
dot = functools.partial(jnp.dot, preferred_element_type=jnp.float32)


def count_pairs(step, layer, li, ri, ti, counts, table):
    for entry in range(16):
        table[0, entry] = 0.0
    live = counts[0, 0, 0, step]
    for p in range(li.shape[4]):
        spot = (ti[0, 0, 0, step, p] ^ layer) * 4 + li[0, 0, 0, step, p] * 2 + ri[0, 0, 0, step, p]
        table[0, spot] = table[0, spot] + jnp.where(p < live, 1.0, 0.0)


def halves(value):
    high = value.astype(jnp.bfloat16)
    return high, (value - high.astype(jnp.float32)).astype(jnp.bfloat16)


def pair_products(left, right_high, right_low, slots):
    count, rows, depth = left.shape
    high, low = halves(left.reshape(count * rows, depth))
    found = []
    for slot in slots:
        both = dot(high, right_high[slot]) + (dot(high, right_low[slot]) + dot(low, right_high[slot]))
        found.append([both[l * rows : (l + 1) * rows] for l in range(count)])
    return found


def combine(found, weight, j, total=None):
    for l in range(2):
        for r in range(2):
            term = found[r][l] * weight(j * 4 + l * 2 + r)
            total = term if total is None else total + term
    return total


def first_kernel(li, ri, ti, counts, left, right, keep, send, table, later):
    layer = lax.axis_index("layer")
    core = layer & 1
    count_pairs(0, layer, li, ri, ti, counts, table)
    count_pairs(1, layer, li, ri, ti, counts, later)
    half = left.shape[1] // 2
    width = send.shape[1]
    parts = [halves(right[slot]) for slot in range(2)]
    highs, lows = [part[0] for part in parts], [part[1] for part in parts]
    for out, side, flip in ((keep, core, 0), (send, 1 - core, 1)):
        begin = pl.multiple_of(side * half, half)
        found = pair_products(left[:, pl.ds(begin, half)], highs, lows, (0, 1))
        for j in range(4):
            spot = j ^ flip
            out[spot * half : (spot + 1) * half, :] = combine(found, lambda k: table[0, k], j)
            for k in range(4):
                row = 4 * half + spot * 4 + k
                out[row : row + 1, :] = jnp.full((1, width), later[0, j * 4 + k], jnp.float32)


def join_kernel(keep, heard, base, weights):
    size = base.shape[0]
    base[...] = keep[:size, :] + heard[:size, :]
    weights[:16] = keep[size:, :]
    weights[16:] = heard[size:, :]


def hold_kernel(*refs):
    for value, out in zip(refs[: len(refs) // 2], refs[len(refs) // 2 :]):
        out[...] = value[...]


def ready_kernel(right_own, right_mate, right_high, right_low):
    for slot in range(4):
        right = (right_own if slot < 2 else right_mate)[slot % 2]
        right_high[slot], right_low[slot] = halves(right)


def second_kernel(left_own, left_mate, right_high, right_low, base, weights, *outs):
    half = left_own.shape[1]
    own = pair_products(left_own[...], right_high, right_low, (0, 1))
    mate = pair_products(left_mate[...], right_high, right_low, (2, 3))
    for j in (2, 3, 1, 0):
        total = combine(own, lambda k: weights[k : k + 1, :], j, base[j * half : (j + 1) * half, :])
        outs[j][...] = combine(mate, lambda k: weights[16 + k : 17 + k, :], j, total)


def last_kernel(mask, chip, far, core, own, out, held, sems):
    side = lax.axis_index("layer") & 1
    scale = mask[0, 0, 0].astype(jnp.float32)
    half = own.shape[0]
    copies = []
    for other, (a, b) in enumerate(((own, chip), (core, far))):
        held[other * half : (other + 1) * half] = (a[...] + b[...]) * scale
        begin = pl.multiple_of((side if other == 0 else 1 - side) * half, half)
        copies.append(pltpu.make_async_copy(held.at[pl.ds(other * half, half)], out.at[pl.ds(begin, half)], sems.at[other]))
        copies[-1].start()
    for copy in copies:
        copy.wait()


def permute(value, to, takes=None):
    names = ("layer", "row", "col")
    sizes = [lax.axis_size(name) for name in names]
    pairs = []
    for l in range(sizes[0]):
        for r in range(sizes[1]):
            for c in range(sizes[2]):
                if takes is not None and not takes(l, r, c):
                    continue
                ln, rn, cn = to(l, r, c)
                pairs.append(((l * sizes[1] + r) * sizes[2] + c, (ln * sizes[1] + rn % sizes[1]) * sizes[2] + cn % sizes[2]))
    return lax.ppermute(value, names, pairs)


def local(left_blocks, right_blocks, left_index, right_index, target_index, live_counts, keep_mask):
    left = left_blocks[0, 0, 0]
    right = right_blocks[0, 0, 0]
    slots, rows, cols = left.shape
    half = rows // 2
    f32 = jnp.float32
    core = lax.axis_index("layer") & 1
    vmem = pl.BlockSpec(memory_space=VMEM)
    smem = pl.BlockSpec(memory_space=SMEM)
    anywhere = pl.BlockSpec(memory_space=pl.ANY)

    def piece(side):
        return lax.dynamic_slice_in_dim(left, side * half, half, 1, allow_negative_indices=False)

    right_first = permute(right, lambda l, r, c: (l, r + 1, c), lambda l, r, c: c == 0)
    left_own = permute(piece(core), lambda l, r, c: (l, r, c + 1))
    left_mate = permute(piece(1 - core), lambda l, r, c: (l ^ 1, r, c + 1))
    within = lax.axis_index("layer") < lax.axis_size("layer")

    def guarded(branch, *args):
        shapes = jax.eval_shape(branch, *args)
        return lax.cond(within, branch, lambda *_: tuple(jnp.zeros(s.shape, s.dtype) for s in shapes), *args)

    def hold(*values):
        return pl.pallas_call(
            hold_kernel,
            out_shape=tuple(jax.ShapeDtypeStruct(v.shape, v.dtype) for v in values),
            in_specs=[vmem] * len(values),
            out_specs=(vmem,) * len(values),
            compiler_params=PARAMS,
            cost_estimate=pl.CostEstimate(flops=1 << 17, bytes_accessed=1 << 20, transcendentals=0),
            name="hold",
        )(*values)

    def early(left, right):
        keep, send = pl.pallas_call(
            first_kernel,
            out_shape=(jax.ShapeDtypeStruct((4 * half + 16, cols), f32),) * 2,
            in_specs=[smem] * 4 + [vmem] * 2,
            out_specs=(vmem, vmem),
            scratch_shapes=[pltpu.SMEM((1, 16), f32)] * 2,
            compiler_params=PARAMS,
            cost_estimate=pl.CostEstimate(flops=6 << 26, bytes_accessed=2 << 20, transcendentals=0),
            name="first_step",
        )(left_index, right_index, target_index, live_counts, left, right)
        heard = permute(send, lambda l, r, c: (l ^ 1, r, c))
        return pl.pallas_call(
            join_kernel,
            out_shape=(jax.ShapeDtypeStruct((4 * half, cols), f32), jax.ShapeDtypeStruct((32, cols), f32)),
            in_specs=[vmem] * 2,
            out_specs=(vmem,) * 2,
            compiler_params=PARAMS,
            cost_estimate=pl.CostEstimate(flops=1 << 17, bytes_accessed=3 << 19, transcendentals=0),
            name="join",
        )(keep, heard)

    def beside(left, right):
        right_rest = permute(right, lambda l, r, c: (l, r + 1, c), lambda l, r, c: c != 0)
        base, weights = guarded(early, left, right)
        base, weights = hold(base, weights)
        (right_rest,) = hold(right_rest)
        return base, weights, right_rest

    def middle(right_first, right_rest):
        right_own = jnp.where(lax.axis_index("col") == 0, right_first, right_rest)
        right_mate = permute(right_own, lambda l, r, c: (l ^ 1, r, c))
        return pl.pallas_call(
            ready_kernel,
            out_shape=(jax.ShapeDtypeStruct((4, rows, cols), jnp.bfloat16),) * 2,
            in_specs=[vmem] * 2,
            out_specs=(vmem,) * 2,
            compiler_params=PARAMS,
            cost_estimate=pl.CostEstimate(flops=1 << 20, bytes_accessed=2 << 20, transcendentals=0),
            name="ready",
        )(right_own, right_mate)

    base, weights, right_rest = guarded(beside, left, right)
    right_high, right_low = guarded(middle, right_first, right_rest)
    own, core_out, chip_out, far_out = pl.pallas_call(
        second_kernel,
        out_shape=(jax.ShapeDtypeStruct((half, cols), f32),) * 4,
        in_specs=[vmem] * 6,
        out_specs=(vmem,) * 4,
        compiler_params=PARAMS,
        cost_estimate=pl.CostEstimate(flops=6 << 26, bytes_accessed=3 << 20, transcendentals=0),
        name="second_step",
    )(left_own, left_mate, right_high, right_low, base, weights)
    chip_in = permute(chip_out, lambda l, r, c: (l ^ 2, r, c))
    far_in = permute(far_out, lambda l, r, c: (l ^ 3, r, c))
    core_in = permute(core_out, lambda l, r, c: (l ^ 1, r, c))
    result = pl.pallas_call(
        last_kernel,
        out_shape=jax.ShapeDtypeStruct((rows, cols), f32),
        in_specs=[smem] + [vmem] * 4,
        out_specs=anywhere,
        scratch_shapes=[pltpu.VMEM((rows, cols), f32), pltpu.SemaphoreType.DMA((2,))],
        compiler_params=PARAMS,
        cost_estimate=pl.CostEstimate(flops=1 << 18, bytes_accessed=1 << 20, transcendentals=0),
        name="last_sum",
    )(keep_mask, chip_in, far_in, core_in, own)
    return result[None, None, None]


def solution(mesh):
    return jax.shard_map(
        local,
        mesh=mesh,
        in_specs=(
            P("layer", "row", "col", None, None, None),
            P("layer", "row", "col", None, None, None),
            P("layer", "row", "col", None, None),
            P("layer", "row", "col", None, None),
            P("layer", "row", "col", None, None),
            P("layer", "row", "col", None),
            P("row", "col", "layer"),
        ),
        out_specs=P("row", "col", "layer", None, None),
        check_vma=False,
    )
```

```python
import functools

import jax
import jax.numpy as jnp
from jax import lax
from jax.experimental import pallas as pl
from jax.experimental.pallas import tpu as pltpu
from jax.sharding import PartitionSpec as P

VMEM = pltpu.VMEM
SMEM = pltpu.SMEM
PARAMS = pltpu.CompilerParams(vmem_limit_bytes=24 << 20)
dot = functools.partial(jnp.dot, preferred_element_type=jnp.float32)


def count_pairs(step, layer, li, ri, ti, counts, table):
    for entry in range(16):
        table[0, entry] = 0.0
    live = counts[0, 0, 0, step]
    for p in range(li.shape[4]):
        spot = (ti[0, 0, 0, step, p] ^ layer) * 4 + li[0, 0, 0, step, p] * 2 + ri[0, 0, 0, step, p]
        table[0, spot] = table[0, spot] + jnp.where(p < live, 1.0, 0.0)


def halves(value):
    high = value.astype(jnp.bfloat16)
    return high, (value - high.astype(jnp.float32)).astype(jnp.bfloat16)


def pair_products(left, right_high, right_low, slots):
    count, rows, depth = left.shape
    high, low = halves(left.reshape(count * rows, depth))
    found = []
    for slot in slots:
        both = dot(high, right_high[slot]) + (dot(high, right_low[slot]) + dot(low, right_high[slot]))
        found.append([both[l * rows : (l + 1) * rows] for l in range(count)])
    return found


def combine(found, weight, j, total=None):
    for l in range(2):
        for r in range(2):
            term = found[r][l] * weight(j * 4 + l * 2 + r)
            total = term if total is None else total + term
    return total


def first_kernel(li, ri, ti, counts, left, right, keep, send, table, later):
    layer = lax.axis_index("layer")
    core = layer & 1
    count_pairs(0, layer, li, ri, ti, counts, table)
    count_pairs(1, layer, li, ri, ti, counts, later)
    half = left.shape[1] // 2
    width = send.shape[1]
    parts = [halves(right[slot]) for slot in range(2)]
    highs, lows = [part[0] for part in parts], [part[1] for part in parts]
    for out, side, flip in ((keep, core, 0), (send, 1 - core, 1)):
        begin = pl.multiple_of(side * half, half)
        found = pair_products(left[:, pl.ds(begin, half)], highs, lows, (0, 1))
        for j in range(4):
            spot = j ^ flip
            out[spot * half : (spot + 1) * half, :] = combine(found, lambda k: table[0, k], j)
            for k in range(4):
                row = 4 * half + spot * 4 + k
                out[row : row + 1, :] = jnp.full((1, width), later[0, j * 4 + k], jnp.float32)


def join_kernel(keep, heard, base, weights):
    size = base.shape[0]
    base[...] = keep[:size, :] + heard[:size, :]
    weights[:16] = keep[size:, :]
    weights[16:] = heard[size:, :]


def split_kernel(left, same, cross):
    side = lax.axis_index("layer") & 1
    half = same.shape[1]
    for out, begin in ((same, side * half), (cross, (1 - side) * half)):
        out[...] = left[:, pl.ds(pl.multiple_of(begin, half), half)]


def hold_kernel(*refs):
    for value, out in zip(refs[: len(refs) // 2], refs[len(refs) // 2 :]):
        out[...] = value[...]


def ready_kernel(right_own, right_mate, right_high, right_low):
    for slot in range(4):
        right = (right_own if slot < 2 else right_mate)[slot % 2]
        right_high[slot], right_low[slot] = halves(right)


def second_kernel(left_own, left_mate, right_high, right_low, base, weights, *outs):
    half = left_own.shape[1]
    own = pair_products(left_own[...], right_high, right_low, (0, 1))
    mate = pair_products(left_mate[...], right_high, right_low, (2, 3))
    for j in (2, 3, 1, 0):
        total = combine(own, lambda k: weights[k : k + 1, :], j, base[j * half : (j + 1) * half, :])
        outs[j][...] = combine(mate, lambda k: weights[16 + k : 17 + k, :], j, total)


def last_kernel(mask, chip, far, core, own, out, held, sems):
    side = lax.axis_index("layer") & 1
    scale = mask[0, 0, 0].astype(jnp.float32)
    half = own.shape[0]
    copies = []
    for other, (a, b) in enumerate(((own, chip), (core, far))):
        held[other * half : (other + 1) * half] = (a[...] + b[...]) * scale
        begin = pl.multiple_of((side if other == 0 else 1 - side) * half, half)
        copies.append(pltpu.make_async_copy(held.at[pl.ds(other * half, half)], out.at[pl.ds(begin, half)], sems.at[other]))
        copies[-1].start()
    for copy in copies:
        copy.wait()


def permute(value, to, takes=None):
    names = ("layer", "row", "col")
    sizes = [lax.axis_size(name) for name in names]
    pairs = []
    for l in range(sizes[0]):
        for r in range(sizes[1]):
            for c in range(sizes[2]):
                if takes is not None and not takes(l, r, c):
                    continue
                ln, rn, cn = to(l, r, c)
                pairs.append(((l * sizes[1] + r) * sizes[2] + c, (ln * sizes[1] + rn % sizes[1]) * sizes[2] + cn % sizes[2]))
    return lax.ppermute(value, names, pairs)


def local(left_blocks, right_blocks, left_index, right_index, target_index, live_counts, keep_mask):
    left = left_blocks[0, 0, 0]
    right = right_blocks[0, 0, 0]
    slots, rows, cols = left.shape
    half = rows // 2
    f32 = jnp.float32
    vmem = pl.BlockSpec(memory_space=VMEM)
    smem = pl.BlockSpec(memory_space=SMEM)
    anywhere = pl.BlockSpec(memory_space=pl.ANY)

    pieces = pl.pallas_call(
        split_kernel,
        out_shape=(jax.ShapeDtypeStruct((slots, half, cols), f32),) * 2,
        in_specs=[vmem],
        out_specs=(vmem,) * 2,
        compiler_params=PARAMS,
        cost_estimate=pl.CostEstimate(flops=1 << 10, bytes_accessed=1 << 20, transcendentals=0),
        name="split",
    )(left)

    last_col = lax.axis_size("col") - 1
    right_first = permute(right, lambda l, r, c: (l, r + 1, c), lambda l, r, c: c != last_col)
    left_own = permute(pieces[0], lambda l, r, c: (l, r, c + 1))
    left_mate = permute(pieces[1], lambda l, r, c: (l ^ 1, r, c + 1))
    within = lax.axis_index("layer") < lax.axis_size("layer")

    def guarded(branch, *args):
        shapes = jax.eval_shape(branch, *args)
        return lax.cond(within, branch, lambda *_: tuple(jnp.zeros(s.shape, s.dtype) for s in shapes), *args)

    def hold(*values):
        return pl.pallas_call(
            hold_kernel,
            out_shape=tuple(jax.ShapeDtypeStruct(v.shape, v.dtype) for v in values),
            in_specs=[vmem] * len(values),
            out_specs=(vmem,) * len(values),
            compiler_params=PARAMS,
            cost_estimate=pl.CostEstimate(flops=1 << 17, bytes_accessed=1 << 20, transcendentals=0),
            name="hold",
        )(*values)

    def early(left, right):
        keep, send = pl.pallas_call(
            first_kernel,
            out_shape=(jax.ShapeDtypeStruct((4 * half + 16, cols), f32),) * 2,
            in_specs=[smem] * 4 + [vmem] * 2,
            out_specs=(vmem, vmem),
            scratch_shapes=[pltpu.SMEM((1, 16), f32)] * 2,
            compiler_params=PARAMS,
            cost_estimate=pl.CostEstimate(flops=6 << 26, bytes_accessed=2 << 20, transcendentals=0),
            name="first_step",
        )(left_index, right_index, target_index, live_counts, left, right)
        heard = permute(send, lambda l, r, c: (l ^ 1, r, c))
        return pl.pallas_call(
            join_kernel,
            out_shape=(jax.ShapeDtypeStruct((4 * half, cols), f32), jax.ShapeDtypeStruct((32, cols), f32)),
            in_specs=[vmem] * 2,
            out_specs=(vmem,) * 2,
            compiler_params=PARAMS,
            cost_estimate=pl.CostEstimate(flops=1 << 17, bytes_accessed=3 << 19, transcendentals=0),
            name="join",
        )(keep, heard)

    def beside(left, right):
        right_rest = permute(right, lambda l, r, c: (l, r + 1, c), lambda l, r, c: c == last_col)
        base, weights = guarded(early, left, right)
        base, weights = hold(base, weights)
        (right_rest,) = hold(right_rest)
        return base, weights, right_rest

    def middle(right_first, right_rest):
        right_own = jnp.where(lax.axis_index("col") == last_col, right_rest, right_first)
        right_mate = permute(right_own, lambda l, r, c: (l ^ 1, r, c))
        return pl.pallas_call(
            ready_kernel,
            out_shape=(jax.ShapeDtypeStruct((4, rows, cols), jnp.bfloat16),) * 2,
            in_specs=[vmem] * 2,
            out_specs=(vmem,) * 2,
            compiler_params=PARAMS,
            cost_estimate=pl.CostEstimate(flops=1 << 20, bytes_accessed=2 << 20, transcendentals=0),
            name="ready",
        )(right_own, right_mate)

    base, weights, right_rest = guarded(beside, left, right)
    right_high, right_low = guarded(middle, right_first, right_rest)
    own, core_out, chip_out, far_out = pl.pallas_call(
        second_kernel,
        out_shape=(jax.ShapeDtypeStruct((half, cols), f32),) * 4,
        in_specs=[vmem] * 6,
        out_specs=(vmem,) * 4,
        compiler_params=PARAMS,
        cost_estimate=pl.CostEstimate(flops=6 << 26, bytes_accessed=3 << 20, transcendentals=0),
        name="second_step",
    )(left_own, left_mate, right_high, right_low, base, weights)
    chip_in = permute(chip_out, lambda l, r, c: (l ^ 2, r, c))
    far_in = permute(far_out, lambda l, r, c: (l ^ 3, r, c))
    core_in = permute(core_out, lambda l, r, c: (l ^ 1, r, c))
    result = pl.pallas_call(
        last_kernel,
        out_shape=jax.ShapeDtypeStruct((rows, cols), f32),
        in_specs=[smem] + [vmem] * 4,
        out_specs=anywhere,
        scratch_shapes=[pltpu.VMEM((rows, cols), f32), pltpu.SemaphoreType.DMA((2,))],
        compiler_params=PARAMS,
        cost_estimate=pl.CostEstimate(flops=1 << 18, bytes_accessed=1 << 20, transcendentals=0),
        name="last_sum",
    )(keep_mask, chip_in, far_in, core_in, own)
    return result[None, None, None]


def solution(mesh):
    return jax.shard_map(
        local,
        mesh=mesh,
        in_specs=(
            P("layer", "row", "col", None, None, None),
            P("layer", "row", "col", None, None, None),
            P("layer", "row", "col", None, None),
            P("layer", "row", "col", None, None),
            P("layer", "row", "col", None, None),
            P("layer", "row", "col", None),
            P("row", "col", "layer"),
        ),
        out_specs=P("row", "col", "layer", None, None),
        check_vma=False,
    )
```

```python
import functools

import jax
import jax.numpy as jnp
from jax import lax
from jax.experimental import pallas as pl
from jax.experimental.pallas import tpu as pltpu
from jax.sharding import PartitionSpec as P

VMEM = pltpu.VMEM
SMEM = pltpu.SMEM
PARAMS = pltpu.CompilerParams(vmem_limit_bytes=24 << 20)
dot = functools.partial(jnp.dot, preferred_element_type=jnp.float32)


def count_pairs(step, layer, li, ri, ti, counts, table):
    for entry in range(16):
        table[0, entry] = 0.0
    live = counts[0, 0, 0, step]
    for p in range(li.shape[4]):
        spot = (ti[0, 0, 0, step, p] ^ layer) * 4 + li[0, 0, 0, step, p] * 2 + ri[0, 0, 0, step, p]
        table[0, spot] = table[0, spot] + jnp.where(p < live, 1.0, 0.0)


def halves(value):
    high = value.astype(jnp.bfloat16)
    return high, (value - high.astype(jnp.float32)).astype(jnp.bfloat16)


def pair_products(left, right_high, right_low, slots):
    count, rows, depth = left.shape
    high, low = halves(left.reshape(count * rows, depth))
    found = []
    for slot in slots:
        both = dot(high, right_high[slot]) + (dot(high, right_low[slot]) + dot(low, right_high[slot]))
        found.append([both[l * rows : (l + 1) * rows] for l in range(count)])
    return found


def combine(found, weight, j, total=None):
    for l in range(2):
        for r in range(2):
            term = found[r][l] * weight(j * 4 + l * 2 + r)
            total = term if total is None else total + term
    return total


def first_kernel(li, ri, ti, counts, left, right, keep, send, table, later):
    layer = lax.axis_index("layer")
    core = layer & 1
    count_pairs(0, layer, li, ri, ti, counts, table)
    count_pairs(1, layer, li, ri, ti, counts, later)
    half = left.shape[1] // 2
    width = send.shape[1]
    parts = [halves(right[slot]) for slot in range(2)]
    highs, lows = [part[0] for part in parts], [part[1] for part in parts]
    for out, side, flip in ((keep, core, 0), (send, 1 - core, 1)):
        begin = pl.multiple_of(side * half, half)
        found = pair_products(left[:, pl.ds(begin, half)], highs, lows, (0, 1))
        for j in range(4):
            spot = j ^ flip
            out[spot * half : (spot + 1) * half, :] = combine(found, lambda k: table[0, k], j)
            for k in range(4):
                row = 4 * half + spot * 4 + k
                out[row : row + 1, :] = jnp.full((1, width), later[0, j * 4 + k], jnp.float32)


def join_kernel(keep, heard, base, weights):
    size = base.shape[0]
    base[...] = keep[:size, :] + heard[:size, :]
    weights[:16] = keep[size:, :]
    weights[16:] = heard[size:, :]


def split_kernel(left, same, cross, held, sems):
    side = lax.axis_index("layer") & 1
    half = same.shape[1]
    copies = [pltpu.make_async_copy(left.at[slot], held.at[slot], sems.at[slot]) for slot in range(2)]
    for copy in copies:
        copy.start()
    for slot in range(2):
        copies[slot].wait()
        for out, begin in ((same, side * half), (cross, (1 - side) * half)):
            out[slot] = held[slot, pl.ds(pl.multiple_of(begin, half), half)]


def hold_kernel(*refs):
    for value, out in zip(refs[: len(refs) // 2], refs[len(refs) // 2 :]):
        out[...] = value[...]


def ready_kernel(right_own, right_mate, right_high, right_low):
    for slot in range(4):
        right = (right_own if slot < 2 else right_mate)[slot % 2]
        right_high[slot], right_low[slot] = halves(right)


def second_kernel(left_own, left_mate, right_high, right_low, base, weights, *outs):
    half = left_own.shape[1]
    own = pair_products(left_own[...], right_high, right_low, (0, 1))
    mate = pair_products(left_mate[...], right_high, right_low, (2, 3))
    for j in (2, 3, 1, 0):
        total = combine(own, lambda k: weights[k : k + 1, :], j, base[j * half : (j + 1) * half, :])
        outs[j][...] = combine(mate, lambda k: weights[16 + k : 17 + k, :], j, total)


def last_kernel(mask, chip, far, core, own, out, held, sems):
    side = lax.axis_index("layer") & 1
    scale = mask[0, 0, 0].astype(jnp.float32)
    half = own.shape[0]
    copies = []
    for other, (a, b) in enumerate(((own, chip), (core, far))):
        held[other * half : (other + 1) * half] = (a[...] + b[...]) * scale
        begin = pl.multiple_of((side if other == 0 else 1 - side) * half, half)
        copies.append(pltpu.make_async_copy(held.at[pl.ds(other * half, half)], out.at[pl.ds(begin, half)], sems.at[other]))
        copies[-1].start()
    for copy in copies:
        copy.wait()


def permute(value, to, takes=None):
    names = ("layer", "row", "col")
    sizes = [lax.axis_size(name) for name in names]
    pairs = []
    for l in range(sizes[0]):
        for r in range(sizes[1]):
            for c in range(sizes[2]):
                if takes is not None and not takes(l, r, c):
                    continue
                ln, rn, cn = to(l, r, c)
                pairs.append(((l * sizes[1] + r) * sizes[2] + c, (ln * sizes[1] + rn % sizes[1]) * sizes[2] + cn % sizes[2]))
    return lax.ppermute(value, names, pairs)


def local(left_blocks, right_blocks, left_index, right_index, target_index, live_counts, keep_mask):
    left = left_blocks[0, 0, 0]
    right = right_blocks[0, 0, 0]
    slots, rows, cols = left.shape
    half = rows // 2
    f32 = jnp.float32
    vmem = pl.BlockSpec(memory_space=VMEM)
    smem = pl.BlockSpec(memory_space=SMEM)
    anywhere = pl.BlockSpec(memory_space=pl.ANY)

    pieces = pl.pallas_call(
        split_kernel,
        out_shape=(jax.ShapeDtypeStruct((slots, half, cols), f32),) * 2,
        in_specs=[anywhere],
        out_specs=(vmem,) * 2,
        scratch_shapes=[pltpu.VMEM((slots, rows, cols), f32), pltpu.SemaphoreType.DMA((2,))],
        compiler_params=PARAMS,
        cost_estimate=pl.CostEstimate(flops=1 << 10, bytes_accessed=1 << 20, transcendentals=0),
        name="split",
    )(left)

    last_col = lax.axis_size("col") - 1
    right_first = permute(right, lambda l, r, c: (l, r + 1, c), lambda l, r, c: c != last_col)
    left_own = permute(pieces[0], lambda l, r, c: (l, r, c + 1))
    left_mate = permute(pieces[1], lambda l, r, c: (l ^ 1, r, c + 1))
    within = lax.axis_index("layer") < lax.axis_size("layer")

    def guarded(branch, *args):
        shapes = jax.eval_shape(branch, *args)
        return lax.cond(within, branch, lambda *_: tuple(jnp.zeros(s.shape, s.dtype) for s in shapes), *args)

    def hold(*values):
        return pl.pallas_call(
            hold_kernel,
            out_shape=tuple(jax.ShapeDtypeStruct(v.shape, v.dtype) for v in values),
            in_specs=[vmem] * len(values),
            out_specs=(vmem,) * len(values),
            compiler_params=PARAMS,
            cost_estimate=pl.CostEstimate(flops=1 << 17, bytes_accessed=1 << 20, transcendentals=0),
            name="hold",
        )(*values)

    def early(left, right):
        keep, send = pl.pallas_call(
            first_kernel,
            out_shape=(jax.ShapeDtypeStruct((4 * half + 16, cols), f32),) * 2,
            in_specs=[smem] * 4 + [vmem] * 2,
            out_specs=(vmem, vmem),
            scratch_shapes=[pltpu.SMEM((1, 16), f32)] * 2,
            compiler_params=PARAMS,
            cost_estimate=pl.CostEstimate(flops=6 << 26, bytes_accessed=2 << 20, transcendentals=0),
            name="first_step",
        )(left_index, right_index, target_index, live_counts, left, right)
        heard = permute(send, lambda l, r, c: (l ^ 1, r, c))
        return pl.pallas_call(
            join_kernel,
            out_shape=(jax.ShapeDtypeStruct((4 * half, cols), f32), jax.ShapeDtypeStruct((32, cols), f32)),
            in_specs=[vmem] * 2,
            out_specs=(vmem,) * 2,
            compiler_params=PARAMS,
            cost_estimate=pl.CostEstimate(flops=1 << 17, bytes_accessed=3 << 19, transcendentals=0),
            name="join",
        )(keep, heard)

    def beside(left, right):
        right_rest = permute(right, lambda l, r, c: (l, r + 1, c), lambda l, r, c: c == last_col)
        base, weights = guarded(early, left, right)
        base, weights = hold(base, weights)
        (right_rest,) = hold(right_rest)
        return base, weights, right_rest

    def middle(right_first, right_rest):
        right_own = jnp.where(lax.axis_index("col") == last_col, right_rest, right_first)
        right_mate = permute(right_own, lambda l, r, c: (l ^ 1, r, c))
        return pl.pallas_call(
            ready_kernel,
            out_shape=(jax.ShapeDtypeStruct((4, rows, cols), jnp.bfloat16),) * 2,
            in_specs=[vmem] * 2,
            out_specs=(vmem,) * 2,
            compiler_params=PARAMS,
            cost_estimate=pl.CostEstimate(flops=1 << 20, bytes_accessed=2 << 20, transcendentals=0),
            name="ready",
        )(right_own, right_mate)

    base, weights, right_rest = guarded(beside, left, right)
    (right_first,) = hold(right_first)
    right_high, right_low = guarded(middle, right_first, right_rest)
    own, core_out, chip_out, far_out = pl.pallas_call(
        second_kernel,
        out_shape=(jax.ShapeDtypeStruct((half, cols), f32),) * 4,
        in_specs=[vmem] * 6,
        out_specs=(vmem,) * 4,
        compiler_params=PARAMS,
        cost_estimate=pl.CostEstimate(flops=6 << 26, bytes_accessed=3 << 20, transcendentals=0),
        name="second_step",
    )(left_own, left_mate, right_high, right_low, base, weights)
    chip_in = permute(chip_out, lambda l, r, c: (l ^ 2, r, c))
    far_in = permute(far_out, lambda l, r, c: (l ^ 3, r, c))
    core_in = permute(core_out, lambda l, r, c: (l ^ 1, r, c))
    result = pl.pallas_call(
        last_kernel,
        out_shape=jax.ShapeDtypeStruct((rows, cols), f32),
        in_specs=[smem] + [vmem] * 4,
        out_specs=anywhere,
        scratch_shapes=[pltpu.VMEM((rows, cols), f32), pltpu.SemaphoreType.DMA((2,))],
        compiler_params=PARAMS,
        cost_estimate=pl.CostEstimate(flops=1 << 18, bytes_accessed=1 << 20, transcendentals=0),
        name="last_sum",
    )(keep_mask, chip_in, far_in, core_in, own)
    return result[None, None, None]


def solution(mesh):
    return jax.shard_map(
        local,
        mesh=mesh,
        in_specs=(
            P("layer", "row", "col", None, None, None),
            P("layer", "row", "col", None, None, None),
            P("layer", "row", "col", None, None),
            P("layer", "row", "col", None, None),
            P("layer", "row", "col", None, None),
            P("layer", "row", "col", None),
            P("row", "col", "layer"),
        ),
        out_specs=P("row", "col", "layer", None, None),
        check_vma=False,
    )
```

```python
import functools

import jax
import jax.numpy as jnp
from jax import lax
from jax.experimental import pallas as pl
from jax.experimental.pallas import tpu as pltpu
from jax.sharding import PartitionSpec as P

VMEM = pltpu.VMEM
SMEM = pltpu.SMEM
PARAMS = pltpu.CompilerParams(vmem_limit_bytes=24 << 20)
dot = functools.partial(jnp.dot, preferred_element_type=jnp.float32)


def count_pairs(step, layer, li, ri, ti, counts, table):
    for entry in range(16):
        table[0, entry] = 0.0
    live = counts[0, 0, 0, step]
    for p in range(li.shape[4]):
        spot = (ti[0, 0, 0, step, p] ^ layer) * 4 + li[0, 0, 0, step, p] * 2 + ri[0, 0, 0, step, p]
        table[0, spot] = table[0, spot] + jnp.where(p < live, 1.0, 0.0)


def halves(value):
    high = value.astype(jnp.bfloat16)
    return high, (value - high.astype(jnp.float32)).astype(jnp.bfloat16)


def pair_products(left, right_high, right_low, slots):
    count, rows, depth = left.shape
    high, low = halves(left.reshape(count * rows, depth))
    found = []
    for slot in slots:
        both = dot(high, right_high[slot]) + (dot(high, right_low[slot]) + dot(low, right_high[slot]))
        found.append([both[l * rows : (l + 1) * rows] for l in range(count)])
    return found


def combine(found, weight, j, total=None):
    for l in range(2):
        for r in range(2):
            term = found[r][l] * weight(j * 4 + l * 2 + r)
            total = term if total is None else total + term
    return total


def first_kernel(li, ri, ti, counts, left, right, keep, send, table, later):
    layer = lax.axis_index("layer")
    core = layer & 1
    count_pairs(0, layer, li, ri, ti, counts, table)
    count_pairs(1, layer, li, ri, ti, counts, later)
    half = left.shape[1] // 2
    width = send.shape[1]
    parts = [halves(right[slot]) for slot in range(2)]
    highs, lows = [part[0] for part in parts], [part[1] for part in parts]
    for out, side, flip in ((keep, core, 0), (send, 1 - core, 1)):
        begin = pl.multiple_of(side * half, half)
        found = pair_products(left[:, pl.ds(begin, half)], highs, lows, (0, 1))
        for j in range(4):
            spot = j ^ flip
            out[spot * half : (spot + 1) * half, :] = combine(found, lambda k: table[0, k], j)
            for k in range(4):
                row = 4 * half + spot * 4 + k
                out[row : row + 1, :] = jnp.full((1, width), later[0, j * 4 + k], jnp.float32)


def join_kernel(keep, heard, base, weights):
    size = base.shape[0]
    base[...] = keep[:size, :] + heard[:size, :]
    weights[:16] = keep[size:, :]
    weights[16:] = heard[size:, :]


def cut_kernel(flip, left, piece, sems):
    half = piece.shape[1]
    side = (lax.axis_index("layer") & 1) ^ flip
    rows = pl.ds(pl.multiple_of(side * half, half), half)
    copies = [pltpu.make_async_copy(left.at[slot, rows], piece.at[slot], sems.at[slot]) for slot in range(2)]
    for copy in copies:
        copy.start()
    for copy in copies:
        copy.wait()


def hold_kernel(*refs):
    for value, out in zip(refs[: len(refs) // 2], refs[len(refs) // 2 :]):
        out[...] = value[...]


def ready_kernel(right_own, right_mate, right_high, right_low):
    for slot in range(4):
        right = (right_own if slot < 2 else right_mate)[slot % 2]
        right_high[slot], right_low[slot] = halves(right)


def own_kernel(left, right_high, right_low, weights, base_far, part, base, sem):
    copy = pltpu.make_async_copy(base_far, base, sem)
    copy.start()
    half = left.shape[1]
    found = pair_products(left[...], right_high, right_low, (0, 1))
    copy.wait()
    for j in range(4):
        rows = slice(j * half, (j + 1) * half)
        part[rows, :] = combine(found, lambda k: weights[k : k + 1, :], j, base[rows, :])


def mate_kernel(left, right_high, right_low, part, weights, *outs):
    half = left.shape[1]
    found = pair_products(left[...], right_high, right_low, (2, 3))
    for j in (2, 3, 1, 0):
        rows = slice(j * half, (j + 1) * half)
        outs[j][...] = combine(found, lambda k: weights[16 + k : 17 + k, :], j, part[rows, :])


def last_kernel(mask, chip, far, core, own, out, held, sems):
    side = lax.axis_index("layer") & 1
    scale = mask[0, 0, 0].astype(jnp.float32)
    half = own.shape[0]
    copies = []
    for other, (a, b) in enumerate(((own, chip), (core, far))):
        held[other * half : (other + 1) * half] = (a[...] + b[...]) * scale
        begin = pl.multiple_of((side if other == 0 else 1 - side) * half, half)
        copies.append(pltpu.make_async_copy(held.at[pl.ds(other * half, half)], out.at[pl.ds(begin, half)], sems.at[other]))
        copies[-1].start()
    for copy in copies:
        copy.wait()


def permute(value, to, takes=None):
    names = ("layer", "row", "col")
    sizes = [lax.axis_size(name) for name in names]
    pairs = []
    for l in range(sizes[0]):
        for r in range(sizes[1]):
            for c in range(sizes[2]):
                if takes is not None and not takes(l, r, c):
                    continue
                ln, rn, cn = to(l, r, c)
                pairs.append(((l * sizes[1] + r) * sizes[2] + c, (ln * sizes[1] + rn % sizes[1]) * sizes[2] + cn % sizes[2]))
    return lax.ppermute(value, names, pairs)


def local(left_blocks, right_blocks, left_index, right_index, target_index, live_counts, keep_mask):
    left = left_blocks[0, 0, 0]
    right = right_blocks[0, 0, 0]
    slots, rows, cols = left.shape
    half = rows // 2
    f32 = jnp.float32
    vmem = pl.BlockSpec(memory_space=VMEM)
    smem = pl.BlockSpec(memory_space=SMEM)
    anywhere = pl.BlockSpec(memory_space=pl.ANY)

    def cut(flip):
        return pl.pallas_call(
            functools.partial(cut_kernel, flip),
            out_shape=jax.ShapeDtypeStruct((slots, half, cols), f32),
            in_specs=[anywhere],
            out_specs=vmem,
            scratch_shapes=[pltpu.SemaphoreType.DMA((2,))],
            compiler_params=PARAMS,
            cost_estimate=pl.CostEstimate(flops=1 << 10, bytes_accessed=1 << 19, transcendentals=0),
            name="cut",
        )(left)

    last_col = lax.axis_size("col") - 1
    right_first = permute(right, lambda l, r, c: (l, r + 1, c), lambda l, r, c: c != last_col)
    same, cross = cut(0), cut(1)
    left_own = permute(same, lambda l, r, c: (l, r, c + 1))
    left_mate = permute(cross, lambda l, r, c: (l ^ 1, r, c + 1))
    within = lax.axis_index("layer") < lax.axis_size("layer")

    def guarded(branch, *args):
        shapes = jax.eval_shape(branch, *args)
        return lax.cond(within, branch, lambda *_: tuple(jnp.zeros(s.shape, s.dtype) for s in shapes), *args)

    def hold(*values):
        return pl.pallas_call(
            hold_kernel,
            out_shape=tuple(jax.ShapeDtypeStruct(v.shape, v.dtype) for v in values),
            in_specs=[vmem] * len(values),
            out_specs=(vmem,) * len(values),
            compiler_params=PARAMS,
            cost_estimate=pl.CostEstimate(flops=1 << 10, bytes_accessed=1 << 10, transcendentals=0),
            name="hold",
        )(*values)

    def early(left, right):
        keep, send = pl.pallas_call(
            first_kernel,
            out_shape=(jax.ShapeDtypeStruct((4 * half + 16, cols), f32),) * 2,
            in_specs=[smem] * 4 + [vmem] * 2,
            out_specs=(vmem, vmem),
            scratch_shapes=[pltpu.SMEM((1, 16), f32)] * 2,
            compiler_params=PARAMS,
            cost_estimate=pl.CostEstimate(flops=6 << 26, bytes_accessed=2 << 20, transcendentals=0),
            name="first_step",
        )(left_index, right_index, target_index, live_counts, left, right)
        heard = permute(send, lambda l, r, c: (l ^ 1, r, c))
        return pl.pallas_call(
            join_kernel,
            out_shape=(jax.ShapeDtypeStruct((4 * half, cols), f32), jax.ShapeDtypeStruct((32, cols), f32)),
            in_specs=[vmem] * 2,
            out_specs=(vmem,) * 2,
            compiler_params=PARAMS,
            cost_estimate=pl.CostEstimate(flops=1 << 17, bytes_accessed=3 << 19, transcendentals=0),
            name="join",
        )(keep, heard)

    def beside(left, right):
        right_rest = permute(right, lambda l, r, c: (l, r + 1, c), lambda l, r, c: c == last_col)
        base, weights = guarded(early, left, right)
        base, weights = hold(base, weights)
        (right_rest,) = hold(right_rest)
        return base, weights, right_rest

    def middle(right_first, right_rest):
        right_own = jnp.where(lax.axis_index("col") == last_col, right_rest, right_first)
        right_mate = permute(right_own, lambda l, r, c: (l ^ 1, r, c))
        return pl.pallas_call(
            ready_kernel,
            out_shape=(jax.ShapeDtypeStruct((4, rows, cols), jnp.bfloat16),) * 2,
            in_specs=[vmem] * 2,
            out_specs=(vmem,) * 2,
            compiler_params=PARAMS,
            cost_estimate=pl.CostEstimate(flops=1 << 10, bytes_accessed=1 << 10, transcendentals=0),
            name="ready",
        )(right_own, right_mate)

    base, weights, right_rest = guarded(beside, left, right)
    (right_first,) = hold(right_first)
    right_high, right_low = guarded(middle, right_first, right_rest)
    part = pl.pallas_call(
        own_kernel,
        out_shape=jax.ShapeDtypeStruct((4 * half, cols), f32),
        in_specs=[vmem] * 4 + [anywhere],
        out_specs=vmem,
        scratch_shapes=[pltpu.VMEM((4 * half, cols), f32), pltpu.SemaphoreType.DMA],
        compiler_params=PARAMS,
        cost_estimate=pl.CostEstimate(flops=3 << 26, bytes_accessed=2 << 20, transcendentals=0),
        name="own_layer",
    )(left_own, right_high, right_low, weights, base)
    own, core_out, chip_out, far_out = pl.pallas_call(
        mate_kernel,
        out_shape=(jax.ShapeDtypeStruct((half, cols), f32),) * 4,
        in_specs=[vmem] * 5,
        out_specs=(vmem,) * 4,
        compiler_params=PARAMS,
        cost_estimate=pl.CostEstimate(flops=3 << 26, bytes_accessed=2 << 20, transcendentals=0),
        name="mate_layer",
    )(left_mate, right_high, right_low, part, weights)
    chip_in = permute(chip_out, lambda l, r, c: (l ^ 2, r, c))
    far_in = permute(far_out, lambda l, r, c: (l ^ 3, r, c))
    core_in = permute(core_out, lambda l, r, c: (l ^ 1, r, c))
    chip_in, far_in = hold(chip_in, far_in)
    result = pl.pallas_call(
        last_kernel,
        out_shape=jax.ShapeDtypeStruct((rows, cols), f32),
        in_specs=[smem] + [vmem] * 4,
        out_specs=anywhere,
        scratch_shapes=[pltpu.VMEM((rows, cols), f32), pltpu.SemaphoreType.DMA((2,))],
        compiler_params=PARAMS,
        cost_estimate=pl.CostEstimate(flops=1 << 18, bytes_accessed=1 << 20, transcendentals=0),
        name="last_sum",
    )(keep_mask, chip_in, far_in, core_in, own)
    return result[None, None, None]


def solution(mesh):
    return jax.shard_map(
        local,
        mesh=mesh,
        in_specs=(
            P("layer", "row", "col", None, None, None),
            P("layer", "row", "col", None, None, None),
            P("layer", "row", "col", None, None),
            P("layer", "row", "col", None, None),
            P("layer", "row", "col", None, None),
            P("layer", "row", "col", None),
            P("row", "col", "layer"),
        ),
        out_specs=P("row", "col", "layer", None, None),
        check_vma=False,
    )
```

```python
import functools

import jax
import jax.numpy as jnp
from jax import lax
from jax.experimental import pallas as pl
from jax.experimental.pallas import tpu as pltpu
from jax.sharding import PartitionSpec as P

VMEM = pltpu.VMEM
SMEM = pltpu.SMEM
PARAMS = pltpu.CompilerParams(vmem_limit_bytes=24 << 20)
dot = functools.partial(jnp.dot, preferred_element_type=jnp.float32)


def count_pairs(step, layer, li, ri, ti, counts, table):
    for entry in range(16):
        table[0, entry] = 0.0
    live = counts[0, 0, 0, step]
    for p in range(li.shape[4]):
        spot = (ti[0, 0, 0, step, p] ^ layer) * 4 + li[0, 0, 0, step, p] * 2 + ri[0, 0, 0, step, p]
        table[0, spot] = table[0, spot] + jnp.where(p < live, 1.0, 0.0)


def halves(value):
    high = value.astype(jnp.bfloat16)
    return high, (value - high.astype(jnp.float32)).astype(jnp.bfloat16)


def pair_products(left, right_high, right_low, slots):
    count, rows, depth = left.shape
    high, low = halves(left.reshape(count * rows, depth))
    found = []
    stacked = jnp.concatenate([high, low], axis=0)
    size = count * rows
    for slot in slots:
        first = dot(stacked, right_high[slot])
        both = first[:size] + (dot(high, right_low[slot]) + first[size:])
        found.append([both[l * rows : (l + 1) * rows] for l in range(count)])
    return found


def combine(found, weight, j, total=None):
    for l in range(2):
        for r in range(2):
            term = found[r][l] * weight(j * 4 + l * 2 + r)
            total = term if total is None else total + term
    return total


def first_kernel(li, ri, ti, counts, left, right, keep, send, table, later):
    layer = lax.axis_index("layer")
    core = layer & 1
    count_pairs(0, layer, li, ri, ti, counts, table)
    count_pairs(1, layer, li, ri, ti, counts, later)
    half = left.shape[1] // 2
    width = send.shape[1]
    parts = [halves(right[slot]) for slot in range(2)]
    highs, lows = [part[0] for part in parts], [part[1] for part in parts]
    for out, side, flip in ((keep, core, 0), (send, 1 - core, 1)):
        begin = pl.multiple_of(side * half, half)
        found = pair_products(left[:, pl.ds(begin, half)], highs, lows, (0, 1))
        for j in range(4):
            spot = j ^ flip
            out[spot * half : (spot + 1) * half, :] = combine(found, lambda k: table[0, k], j)
            for k in range(4):
                row = 4 * half + spot * 4 + k
                out[row : row + 1, :] = jnp.full((1, width), later[0, j * 4 + k], jnp.float32)


def join_kernel(keep, heard, base, weights):
    size = base.shape[0]
    base[...] = keep[:size, :] + heard[:size, :]
    weights[:16] = keep[size:, :]
    weights[16:] = heard[size:, :]


def split_kernel(left, same, cross, held, sems):
    side = lax.axis_index("layer") & 1
    half = same.shape[1]
    copies = [pltpu.make_async_copy(left.at[slot], held.at[slot], sems.at[slot]) for slot in range(2)]
    for copy in copies:
        copy.start()
    for slot in range(2):
        copies[slot].wait()
        for out, begin in ((same, side * half), (cross, (1 - side) * half)):
            out[slot] = held[slot, pl.ds(pl.multiple_of(begin, half), half)]


def hold_kernel(*refs):
    for value, out in zip(refs[: len(refs) // 2], refs[len(refs) // 2 :]):
        out[...] = value[...]


def ready_kernel(right_own, right_mate, right_high, right_low):
    for slot in range(4):
        right = (right_own if slot < 2 else right_mate)[slot % 2]
        right_high[slot], right_low[slot] = halves(right)


def own_kernel(left, right_high, right_low, base, weights, part):
    half = left.shape[1]
    found = pair_products(left[...], right_high, right_low, (0, 1))
    for j in range(4):
        rows = slice(j * half, (j + 1) * half)
        part[rows, :] = combine(found, lambda k: weights[k : k + 1, :], j, base[rows, :])


def mate_kernel(left, right_high, right_low, part, weights, *outs):
    half = left.shape[1]
    found = pair_products(left[...], right_high, right_low, (2, 3))
    for j in (2, 3, 1, 0):
        rows = slice(j * half, (j + 1) * half)
        outs[j][...] = combine(found, lambda k: weights[16 + k : 17 + k, :], j, part[rows, :])


def last_kernel(mask, chip, far, core, own, out, held, sems):
    side = lax.axis_index("layer") & 1
    scale = mask[0, 0, 0].astype(jnp.float32)
    half = own.shape[0]
    copies = []
    for other, (a, b) in enumerate(((own, chip), (core, far))):
        held[other * half : (other + 1) * half] = (a[...] + b[...]) * scale
        begin = pl.multiple_of((side if other == 0 else 1 - side) * half, half)
        copies.append(pltpu.make_async_copy(held.at[pl.ds(other * half, half)], out.at[pl.ds(begin, half)], sems.at[other]))
        copies[-1].start()
    for copy in copies:
        copy.wait()


def permute(value, to, takes=None):
    names = ("layer", "row", "col")
    sizes = [lax.axis_size(name) for name in names]
    pairs = []
    for l in range(sizes[0]):
        for r in range(sizes[1]):
            for c in range(sizes[2]):
                if takes is not None and not takes(l, r, c):
                    continue
                ln, rn, cn = to(l, r, c)
                pairs.append(((l * sizes[1] + r) * sizes[2] + c, (ln * sizes[1] + rn % sizes[1]) * sizes[2] + cn % sizes[2]))
    return lax.ppermute(value, names, pairs)


def local(left_blocks, right_blocks, left_index, right_index, target_index, live_counts, keep_mask):
    left = left_blocks[0, 0, 0]
    right = right_blocks[0, 0, 0]
    slots, rows, cols = left.shape
    half = rows // 2
    f32 = jnp.float32
    vmem = pl.BlockSpec(memory_space=VMEM)
    smem = pl.BlockSpec(memory_space=SMEM)
    anywhere = pl.BlockSpec(memory_space=pl.ANY)

    pieces = pl.pallas_call(
        split_kernel,
        out_shape=(jax.ShapeDtypeStruct((slots, half, cols), f32),) * 2,
        in_specs=[anywhere],
        out_specs=(vmem,) * 2,
        scratch_shapes=[pltpu.VMEM((slots, rows, cols), f32), pltpu.SemaphoreType.DMA((2,))],
        compiler_params=PARAMS,
        cost_estimate=pl.CostEstimate(flops=1 << 10, bytes_accessed=1 << 20, transcendentals=0),
        name="split",
    )(left)

    last_col = lax.axis_size("col") - 1
    right_first = permute(right, lambda l, r, c: (l, r + 1, c), lambda l, r, c: c != last_col)
    left_own = permute(pieces[0], lambda l, r, c: (l, r, c + 1))
    left_mate = permute(pieces[1], lambda l, r, c: (l ^ 1, r, c + 1))
    within = lax.axis_index("layer") < lax.axis_size("layer")

    def guarded(branch, *args):
        shapes = jax.eval_shape(branch, *args)
        return lax.cond(within, branch, lambda *_: tuple(jnp.zeros(s.shape, s.dtype) for s in shapes), *args)

    def hold(*values):
        return pl.pallas_call(
            hold_kernel,
            out_shape=tuple(jax.ShapeDtypeStruct(v.shape, v.dtype) for v in values),
            in_specs=[vmem] * len(values),
            out_specs=(vmem,) * len(values),
            compiler_params=PARAMS,
            cost_estimate=pl.CostEstimate(flops=1 << 17, bytes_accessed=1 << 20, transcendentals=0),
            name="hold",
        )(*values)

    def early(left, right):
        keep, send = pl.pallas_call(
            first_kernel,
            out_shape=(jax.ShapeDtypeStruct((4 * half + 16, cols), f32),) * 2,
            in_specs=[smem] * 4 + [vmem] * 2,
            out_specs=(vmem, vmem),
            scratch_shapes=[pltpu.SMEM((1, 16), f32)] * 2,
            compiler_params=PARAMS,
            cost_estimate=pl.CostEstimate(flops=6 << 26, bytes_accessed=2 << 20, transcendentals=0),
            name="first_step",
        )(left_index, right_index, target_index, live_counts, left, right)
        heard = permute(send, lambda l, r, c: (l ^ 1, r, c))
        return pl.pallas_call(
            join_kernel,
            out_shape=(jax.ShapeDtypeStruct((4 * half, cols), f32), jax.ShapeDtypeStruct((32, cols), f32)),
            in_specs=[vmem] * 2,
            out_specs=(vmem,) * 2,
            compiler_params=PARAMS,
            cost_estimate=pl.CostEstimate(flops=1 << 17, bytes_accessed=3 << 19, transcendentals=0),
            name="join",
        )(keep, heard)

    def beside(left, right):
        right_rest = permute(right, lambda l, r, c: (l, r + 1, c), lambda l, r, c: c == last_col)
        base, weights = guarded(early, left, right)
        base, weights = hold(base, weights)
        (right_rest,) = hold(right_rest)
        return base, weights, right_rest

    def middle(right_first, right_rest):
        right_own = jnp.where(lax.axis_index("col") == last_col, right_rest, right_first)
        right_mate = permute(right_own, lambda l, r, c: (l ^ 1, r, c))
        return pl.pallas_call(
            ready_kernel,
            out_shape=(jax.ShapeDtypeStruct((4, rows, cols), jnp.bfloat16),) * 2,
            in_specs=[vmem] * 2,
            out_specs=(vmem,) * 2,
            compiler_params=PARAMS,
            cost_estimate=pl.CostEstimate(flops=1 << 20, bytes_accessed=2 << 20, transcendentals=0),
            name="ready",
        )(right_own, right_mate)

    base, weights, right_rest = guarded(beside, left, right)
    (right_first,) = hold(right_first)
    base, weights = hold(base, weights)
    right_high, right_low = guarded(middle, right_first, right_rest)
    part = pl.pallas_call(
        own_kernel,
        out_shape=jax.ShapeDtypeStruct((4 * half, cols), f32),
        in_specs=[vmem] * 5,
        out_specs=vmem,
        compiler_params=PARAMS,
        cost_estimate=pl.CostEstimate(flops=3 << 26, bytes_accessed=2 << 20, transcendentals=0),
        name="own_layer",
    )(left_own, right_high, right_low, base, weights)
    own, core_out, chip_out, far_out = pl.pallas_call(
        mate_kernel,
        out_shape=(jax.ShapeDtypeStruct((half, cols), f32),) * 4,
        in_specs=[vmem] * 5,
        out_specs=(vmem,) * 4,
        compiler_params=PARAMS,
        cost_estimate=pl.CostEstimate(flops=3 << 26, bytes_accessed=2 << 20, transcendentals=0),
        name="mate_layer",
    )(left_mate, right_high, right_low, part, weights)
    chip_in = permute(chip_out, lambda l, r, c: (l ^ 2, r, c))
    far_in = permute(far_out, lambda l, r, c: (l ^ 3, r, c))
    core_in = permute(core_out, lambda l, r, c: (l ^ 1, r, c))
    chip_in, far_in = hold(chip_in, far_in)
    result = pl.pallas_call(
        last_kernel,
        out_shape=jax.ShapeDtypeStruct((rows, cols), f32),
        in_specs=[smem] + [vmem] * 4,
        out_specs=anywhere,
        scratch_shapes=[pltpu.VMEM((rows, cols), f32), pltpu.SemaphoreType.DMA((2,))],
        compiler_params=PARAMS,
        cost_estimate=pl.CostEstimate(flops=1 << 18, bytes_accessed=1 << 20, transcendentals=0),
        name="last_sum",
    )(keep_mask, chip_in, far_in, core_in, own)
    return result[None, None, None]


def solution(mesh):
    return jax.shard_map(
        local,
        mesh=mesh,
        in_specs=(
            P("layer", "row", "col", None, None, None),
            P("layer", "row", "col", None, None, None),
            P("layer", "row", "col", None, None),
            P("layer", "row", "col", None, None),
            P("layer", "row", "col", None, None),
            P("layer", "row", "col", None),
            P("row", "col", "layer"),
        ),
        out_specs=P("row", "col", "layer", None, None),
        check_vma=False,
    )
```

```python
import functools

import jax
import jax.numpy as jnp
from jax import lax
from jax.experimental import pallas as pl
from jax.experimental.pallas import tpu as pltpu
from jax.sharding import PartitionSpec as P

VMEM = pltpu.VMEM
SMEM = pltpu.SMEM
PARAMS = pltpu.CompilerParams(vmem_limit_bytes=24 << 20)
dot = functools.partial(jnp.dot, preferred_element_type=jnp.float32)


def count_pairs(step, layer, li, ri, ti, counts, table):
    for entry in range(16):
        table[0, entry] = 0.0
    live = counts[0, 0, 0, step]
    for p in range(li.shape[4]):
        spot = (ti[0, 0, 0, step, p] ^ layer) * 4 + li[0, 0, 0, step, p] * 2 + ri[0, 0, 0, step, p]
        table[0, spot] = table[0, spot] + jnp.where(p < live, 1.0, 0.0)


def halves(value):
    high = value.astype(jnp.bfloat16)
    return high, (value - high.astype(jnp.float32)).astype(jnp.bfloat16)


def pair_products(left, right_high, right_low, slots):
    count, rows, depth = left.shape
    high, low = halves(left.reshape(count * rows, depth))
    found = []
    stacked = jnp.concatenate([high, low], axis=0)
    size = count * rows
    for slot in slots:
        first = dot(stacked, right_high[slot])
        both = first[:size] + (dot(high, right_low[slot]) + first[size:])
        found.append([both[l * rows : (l + 1) * rows] for l in range(count)])
    return found


def combine(found, weight, j, total=None):
    for l in range(2):
        for r in range(2):
            term = found[r][l] * weight(j * 4 + l * 2 + r)
            total = term if total is None else total + term
    return total


def first_kernel(li, ri, ti, counts, left, right, keep, send, table, later):
    layer = lax.axis_index("layer")
    core = layer & 1
    count_pairs(0, layer, li, ri, ti, counts, table)
    count_pairs(1, layer, li, ri, ti, counts, later)
    half = left.shape[1] // 2
    width = send.shape[1]
    parts = [halves(right[slot]) for slot in range(2)]
    highs, lows = [part[0] for part in parts], [part[1] for part in parts]
    for out, side, flip in ((keep, core, 0), (send, 1 - core, 1)):
        begin = pl.multiple_of(side * half, half)
        found = pair_products(left[:, pl.ds(begin, half)], highs, lows, (0, 1))
        for j in range(4):
            spot = j ^ flip
            out[spot * half : (spot + 1) * half, :] = combine(found, lambda k: table[0, k], j)
            for k in range(4):
                row = 4 * half + spot * 4 + k
                out[row : row + 1, :] = jnp.full((1, width), later[0, j * 4 + k], jnp.float32)


def join_kernel(keep, heard, base, weights):
    size = base.shape[0]
    base[...] = keep[:size, :] + heard[:size, :]
    weights[:16] = keep[size:, :]
    weights[16:] = heard[size:, :]


def split_kernel(left, same, cross, held, sems):
    side = lax.axis_index("layer") & 1
    half = same.shape[1]
    copies = [pltpu.make_async_copy(left.at[slot], held.at[slot], sems.at[slot]) for slot in range(2)]
    for copy in copies:
        copy.start()
    for slot in range(2):
        copies[slot].wait()
        for out, begin in ((same, side * half), (cross, (1 - side) * half)):
            out[slot] = held[slot, pl.ds(pl.multiple_of(begin, half), half)]


def hold_kernel(*refs):
    for value, out in zip(refs[: len(refs) // 2], refs[len(refs) // 2 :]):
        out[...] = value[...]


def ready_kernel(right_own, right_mate, right_high, right_low):
    for slot in range(4):
        right = (right_own if slot < 2 else right_mate)[slot % 2]
        right_high[slot], right_low[slot] = halves(right)


def own_kernel(left, right_high, right_low, base, weights, part):
    half = left.shape[1]
    found = pair_products(left[...], right_high, right_low, (0, 1))
    for j in range(4):
        rows = slice(j * half, (j + 1) * half)
        part[rows, :] = combine(found, lambda k: weights[k : k + 1, :], j, base[rows, :])


def mate_kernel(blocks, left, right_high, right_low, part, weights, *outs):
    half = left.shape[1]
    found = pair_products(left[...], right_high, right_low, (2, 3))
    for j, out in zip(blocks, outs):
        out[...] = combine(found, lambda k: weights[16 + k : 17 + k, :], j, part[j * half : (j + 1) * half, :])


def last_kernel(mask, chip, far, core, own, out, held, sems):
    side = lax.axis_index("layer") & 1
    scale = mask[0, 0, 0].astype(jnp.float32)
    half = own.shape[0]
    copies = []
    for other, (a, b) in enumerate(((own, chip), (core, far))):
        held[other * half : (other + 1) * half] = (a[...] + b[...]) * scale
        begin = pl.multiple_of((side if other == 0 else 1 - side) * half, half)
        copies.append(pltpu.make_async_copy(held.at[pl.ds(other * half, half)], out.at[pl.ds(begin, half)], sems.at[other]))
        copies[-1].start()
    for copy in copies:
        copy.wait()


def permute(value, to, takes=None):
    names = ("layer", "row", "col")
    sizes = [lax.axis_size(name) for name in names]
    pairs = []
    for l in range(sizes[0]):
        for r in range(sizes[1]):
            for c in range(sizes[2]):
                if takes is not None and not takes(l, r, c):
                    continue
                ln, rn, cn = to(l, r, c)
                pairs.append(((l * sizes[1] + r) * sizes[2] + c, (ln * sizes[1] + rn % sizes[1]) * sizes[2] + cn % sizes[2]))
    return lax.ppermute(value, names, pairs)


def local(left_blocks, right_blocks, left_index, right_index, target_index, live_counts, keep_mask):
    left = left_blocks[0, 0, 0]
    right = right_blocks[0, 0, 0]
    slots, rows, cols = left.shape
    half = rows // 2
    f32 = jnp.float32
    vmem = pl.BlockSpec(memory_space=VMEM)
    smem = pl.BlockSpec(memory_space=SMEM)
    anywhere = pl.BlockSpec(memory_space=pl.ANY)

    pieces = pl.pallas_call(
        split_kernel,
        out_shape=(jax.ShapeDtypeStruct((slots, half, cols), f32),) * 2,
        in_specs=[anywhere],
        out_specs=(vmem,) * 2,
        scratch_shapes=[pltpu.VMEM((slots, rows, cols), f32), pltpu.SemaphoreType.DMA((2,))],
        compiler_params=PARAMS,
        cost_estimate=pl.CostEstimate(flops=1 << 10, bytes_accessed=1 << 20, transcendentals=0),
        name="split",
    )(left)

    last_col = lax.axis_size("col") - 1
    right_first = permute(right, lambda l, r, c: (l, r + 1, c), lambda l, r, c: c != last_col)
    left_own = permute(pieces[0], lambda l, r, c: (l, r, c + 1))
    left_mate = permute(pieces[1], lambda l, r, c: (l ^ 1, r, c + 1))
    within = lax.axis_index("layer") < lax.axis_size("layer")

    def guarded(branch, *args):
        shapes = jax.eval_shape(branch, *args)
        return lax.cond(within, branch, lambda *_: tuple(jnp.zeros(s.shape, s.dtype) for s in shapes), *args)

    def hold(*values):
        return pl.pallas_call(
            hold_kernel,
            out_shape=tuple(jax.ShapeDtypeStruct(v.shape, v.dtype) for v in values),
            in_specs=[vmem] * len(values),
            out_specs=(vmem,) * len(values),
            compiler_params=PARAMS,
            cost_estimate=pl.CostEstimate(flops=1 << 17, bytes_accessed=1 << 20, transcendentals=0),
            name="hold",
        )(*values)

    def early(left, right):
        keep, send = pl.pallas_call(
            first_kernel,
            out_shape=(jax.ShapeDtypeStruct((4 * half + 16, cols), f32),) * 2,
            in_specs=[smem] * 4 + [vmem] * 2,
            out_specs=(vmem, vmem),
            scratch_shapes=[pltpu.SMEM((1, 16), f32)] * 2,
            compiler_params=PARAMS,
            cost_estimate=pl.CostEstimate(flops=6 << 26, bytes_accessed=2 << 20, transcendentals=0),
            name="first_step",
        )(left_index, right_index, target_index, live_counts, left, right)
        heard = permute(send, lambda l, r, c: (l ^ 1, r, c))
        return pl.pallas_call(
            join_kernel,
            out_shape=(jax.ShapeDtypeStruct((4 * half, cols), f32), jax.ShapeDtypeStruct((32, cols), f32)),
            in_specs=[vmem] * 2,
            out_specs=(vmem,) * 2,
            compiler_params=PARAMS,
            cost_estimate=pl.CostEstimate(flops=1 << 17, bytes_accessed=3 << 19, transcendentals=0),
            name="join",
        )(keep, heard)

    def beside(left, right):
        right_rest = permute(right, lambda l, r, c: (l, r + 1, c), lambda l, r, c: c == last_col)
        base, weights = guarded(early, left, right)
        base, weights = hold(base, weights)
        (right_rest,) = hold(right_rest)
        return base, weights, right_rest

    def middle(right_first, right_rest):
        right_own = jnp.where(lax.axis_index("col") == last_col, right_rest, right_first)
        right_mate = permute(right_own, lambda l, r, c: (l ^ 1, r, c))
        return pl.pallas_call(
            ready_kernel,
            out_shape=(jax.ShapeDtypeStruct((4, rows, cols), jnp.bfloat16),) * 2,
            in_specs=[vmem] * 2,
            out_specs=(vmem,) * 2,
            compiler_params=PARAMS,
            cost_estimate=pl.CostEstimate(flops=1 << 20, bytes_accessed=2 << 20, transcendentals=0),
            name="ready",
        )(right_own, right_mate)

    base, weights, right_rest = guarded(beside, left, right)
    (right_first,) = hold(right_first)
    base, weights = hold(base, weights)
    right_high, right_low = guarded(middle, right_first, right_rest)
    part = pl.pallas_call(
        own_kernel,
        out_shape=jax.ShapeDtypeStruct((4 * half, cols), f32),
        in_specs=[vmem] * 5,
        out_specs=vmem,
        compiler_params=PARAMS,
        cost_estimate=pl.CostEstimate(flops=3 << 26, bytes_accessed=2 << 20, transcendentals=0),
        name="own_layer",
    )(left_own, right_high, right_low, base, weights)
    def mate(*blocks):
        return pl.pallas_call(
            functools.partial(mate_kernel, blocks),
            out_shape=(jax.ShapeDtypeStruct((half, cols), f32),) * 2,
            in_specs=[vmem] * 5,
            out_specs=(vmem,) * 2,
            compiler_params=PARAMS,
            cost_estimate=pl.CostEstimate(flops=3 << 26, bytes_accessed=2 << 20, transcendentals=0),
            name="mate_layer",
        )(left_mate, right_high, right_low, part, weights)

    chip_out, far_out = mate(2, 3)
    own, core_out = mate(0, 1)
    chip_in = permute(chip_out, lambda l, r, c: (l ^ 2, r, c))
    far_in = permute(far_out, lambda l, r, c: (l ^ 3, r, c))
    core_in = permute(core_out, lambda l, r, c: (l ^ 1, r, c))
    chip_in, far_in = hold(chip_in, far_in)
    result = pl.pallas_call(
        last_kernel,
        out_shape=jax.ShapeDtypeStruct((rows, cols), f32),
        in_specs=[smem] + [vmem] * 4,
        out_specs=anywhere,
        scratch_shapes=[pltpu.VMEM((rows, cols), f32), pltpu.SemaphoreType.DMA((2,))],
        compiler_params=PARAMS,
        cost_estimate=pl.CostEstimate(flops=1 << 18, bytes_accessed=1 << 20, transcendentals=0),
        name="last_sum",
    )(keep_mask, chip_in, far_in, core_in, own)
    return result[None, None, None]


def solution(mesh):
    return jax.shard_map(
        local,
        mesh=mesh,
        in_specs=(
            P("layer", "row", "col", None, None, None),
            P("layer", "row", "col", None, None, None),
            P("layer", "row", "col", None, None),
            P("layer", "row", "col", None, None),
            P("layer", "row", "col", None, None),
            P("layer", "row", "col", None),
            P("row", "col", "layer"),
        ),
        out_specs=P("row", "col", "layer", None, None),
        check_vma=False,
    )
```

```python
import functools

import jax
import jax.numpy as jnp
from jax import lax
from jax.experimental import pallas as pl
from jax.experimental.pallas import tpu as pltpu
from jax.sharding import PartitionSpec as P

VMEM = pltpu.VMEM
SMEM = pltpu.SMEM
PARAMS = pltpu.CompilerParams(vmem_limit_bytes=24 << 20)
dot = functools.partial(jnp.dot, preferred_element_type=jnp.float32)


def count_pairs(step, layer, li, ri, ti, counts, table):
    for entry in range(16):
        table[0, entry] = 0.0
    live = counts[0, 0, 0, step]
    for p in range(li.shape[4]):
        spot = (ti[0, 0, 0, step, p] ^ layer) * 4 + li[0, 0, 0, step, p] * 2 + ri[0, 0, 0, step, p]
        table[0, spot] = table[0, spot] + jnp.where(p < live, 1.0, 0.0)


def halves(value):
    high = value.astype(jnp.bfloat16)
    return high, (value - high.astype(jnp.float32)).astype(jnp.bfloat16)


def pair_products(left, right_high, right_low, slots):
    count, rows, depth = left.shape
    high, low = halves(left.reshape(count * rows, depth))
    found = []
    stacked = jnp.concatenate([high, low], axis=0)
    size = count * rows
    for slot in slots:
        first = dot(stacked, right_high[slot])
        both = first[:size] + (dot(high, right_low[slot]) + first[size:])
        found.append([both[l * rows : (l + 1) * rows] for l in range(count)])
    return found


def combine(found, weight, j, total=None):
    for l in range(2):
        for r in range(2):
            term = found[r][l] * weight(j * 4 + l * 2 + r)
            total = term if total is None else total + term
    return total


def first_kernel(li, ri, ti, counts, left, right, keep, send, table, later):
    layer = lax.axis_index("layer")
    core = layer & 1
    count_pairs(0, layer, li, ri, ti, counts, table)
    count_pairs(1, layer, li, ri, ti, counts, later)
    half = left.shape[1] // 2
    width = send.shape[1]
    parts = [halves(right[slot]) for slot in range(2)]
    highs, lows = [part[0] for part in parts], [part[1] for part in parts]
    for out, side, flip in ((keep, core, 0), (send, 1 - core, 1)):
        begin = pl.multiple_of(side * half, half)
        found = pair_products(left[:, pl.ds(begin, half)], highs, lows, (0, 1))
        for j in range(4):
            spot = j ^ flip
            out[spot * half : (spot + 1) * half, :] = combine(found, lambda k: table[0, k], j)
            for k in range(4):
                row = 4 * half + spot * 4 + k
                out[row : row + 1, :] = jnp.full((1, width), later[0, j * 4 + k], jnp.float32)


def join_kernel(keep, heard, base, weights):
    size = base.shape[0]
    base[...] = keep[:size, :] + heard[:size, :]
    weights[:16] = keep[size:, :]
    weights[16:] = heard[size:, :]


def split_kernel(left, same, cross, sems):
    side = lax.axis_index("layer") & 1
    half = same.shape[1]
    copies = []
    for out, half_at in ((same, side), (cross, 1 - side)):
        rows = pl.ds(pl.multiple_of(half_at * half, half), half)
        for slot in range(2):
            copies.append(pltpu.make_async_copy(left.at[slot, rows], out.at[slot], sems.at[len(copies)]))
            copies[-1].start()
    for copy in copies:
        copy.wait()


def hold_kernel(*refs):
    for value, out in zip(refs[: len(refs) // 2], refs[len(refs) // 2 :]):
        out[...] = value[...]


def ready_kernel(right_own, right_mate, right_high, right_low):
    for slot in range(4):
        right = (right_own if slot < 2 else right_mate)[slot % 2]
        right_high[slot], right_low[slot] = halves(right)


def own_kernel(left, right_high, right_low, base, weights, part):
    half = left.shape[1]
    found = pair_products(left[...], right_high, right_low, (0, 1))
    for j in range(4):
        rows = slice(j * half, (j + 1) * half)
        part[rows, :] = combine(found, lambda k: weights[k : k + 1, :], j, base[rows, :])


def mate_kernel(left, right_high, right_low, part, weights, *outs):
    half = left.shape[1]
    found = pair_products(left[...], right_high, right_low, (2, 3))
    for j in (2, 3, 1, 0):
        rows = slice(j * half, (j + 1) * half)
        outs[j][...] = combine(found, lambda k: weights[16 + k : 17 + k, :], j, part[rows, :])


def last_kernel(mask, chip, far, core, own, out, held, sems):
    side = lax.axis_index("layer") & 1
    scale = mask[0, 0, 0].astype(jnp.float32)
    half = own.shape[0]
    copies = []
    for other, (a, b) in enumerate(((own, chip), (core, far))):
        held[other * half : (other + 1) * half] = (a[...] + b[...]) * scale
        begin = pl.multiple_of((side if other == 0 else 1 - side) * half, half)
        copies.append(pltpu.make_async_copy(held.at[pl.ds(other * half, half)], out.at[pl.ds(begin, half)], sems.at[other]))
        copies[-1].start()
    for copy in copies:
        copy.wait()


def permute(value, to, takes=None):
    names = ("layer", "row", "col")
    sizes = [lax.axis_size(name) for name in names]
    pairs = []
    for l in range(sizes[0]):
        for r in range(sizes[1]):
            for c in range(sizes[2]):
                if takes is not None and not takes(l, r, c):
                    continue
                ln, rn, cn = to(l, r, c)
                pairs.append(((l * sizes[1] + r) * sizes[2] + c, (ln * sizes[1] + rn % sizes[1]) * sizes[2] + cn % sizes[2]))
    return lax.ppermute(value, names, pairs)


def local(left_blocks, right_blocks, left_index, right_index, target_index, live_counts, keep_mask):
    left = left_blocks[0, 0, 0]
    right = right_blocks[0, 0, 0]
    slots, rows, cols = left.shape
    half = rows // 2
    f32 = jnp.float32
    vmem = pl.BlockSpec(memory_space=VMEM)
    smem = pl.BlockSpec(memory_space=SMEM)
    anywhere = pl.BlockSpec(memory_space=pl.ANY)

    pieces = pl.pallas_call(
        split_kernel,
        out_shape=(jax.ShapeDtypeStruct((slots, half, cols), f32),) * 2,
        in_specs=[anywhere],
        out_specs=(vmem,) * 2,
        scratch_shapes=[pltpu.SemaphoreType.DMA((4,))],
        compiler_params=PARAMS,
        cost_estimate=pl.CostEstimate(flops=1 << 10, bytes_accessed=1 << 20, transcendentals=0),
        name="split",
    )(left)

    last_col = lax.axis_size("col") - 1
    right_first = permute(right, lambda l, r, c: (l, r + 1, c), lambda l, r, c: c != last_col)
    left_own = permute(pieces[0], lambda l, r, c: (l, r, c + 1))
    left_mate = permute(pieces[1], lambda l, r, c: (l ^ 1, r, c + 1))
    within = lax.axis_index("layer") < lax.axis_size("layer")

    def guarded(branch, *args):
        shapes = jax.eval_shape(branch, *args)
        return lax.cond(within, branch, lambda *_: tuple(jnp.zeros(s.shape, s.dtype) for s in shapes), *args)

    def hold(*values):
        return pl.pallas_call(
            hold_kernel,
            out_shape=tuple(jax.ShapeDtypeStruct(v.shape, v.dtype) for v in values),
            in_specs=[vmem] * len(values),
            out_specs=(vmem,) * len(values),
            compiler_params=PARAMS,
            cost_estimate=pl.CostEstimate(flops=1 << 17, bytes_accessed=1 << 20, transcendentals=0),
            name="hold",
        )(*values)

    def early(left, right):
        keep, send = pl.pallas_call(
            first_kernel,
            out_shape=(jax.ShapeDtypeStruct((4 * half + 16, cols), f32),) * 2,
            in_specs=[smem] * 4 + [vmem] * 2,
            out_specs=(vmem, vmem),
            scratch_shapes=[pltpu.SMEM((1, 16), f32)] * 2,
            compiler_params=PARAMS,
            cost_estimate=pl.CostEstimate(flops=6 << 26, bytes_accessed=2 << 20, transcendentals=0),
            name="first_step",
        )(left_index, right_index, target_index, live_counts, left, right)
        heard = permute(send, lambda l, r, c: (l ^ 1, r, c))
        return pl.pallas_call(
            join_kernel,
            out_shape=(jax.ShapeDtypeStruct((4 * half, cols), f32), jax.ShapeDtypeStruct((32, cols), f32)),
            in_specs=[vmem] * 2,
            out_specs=(vmem,) * 2,
            compiler_params=PARAMS,
            cost_estimate=pl.CostEstimate(flops=1 << 17, bytes_accessed=3 << 19, transcendentals=0),
            name="join",
        )(keep, heard)

    def beside(left, right):
        right_rest = permute(right, lambda l, r, c: (l, r + 1, c), lambda l, r, c: c == last_col)
        base, weights = guarded(early, left, right)
        base, weights = hold(base, weights)
        (right_rest,) = hold(right_rest)
        return base, weights, right_rest

    def middle(right_first, right_rest):
        right_own = jnp.where(lax.axis_index("col") == last_col, right_rest, right_first)
        right_mate = permute(right_own, lambda l, r, c: (l ^ 1, r, c))
        return pl.pallas_call(
            ready_kernel,
            out_shape=(jax.ShapeDtypeStruct((4, rows, cols), jnp.bfloat16),) * 2,
            in_specs=[vmem] * 2,
            out_specs=(vmem,) * 2,
            compiler_params=PARAMS,
            cost_estimate=pl.CostEstimate(flops=1 << 20, bytes_accessed=2 << 20, transcendentals=0),
            name="ready",
        )(right_own, right_mate)

    base, weights, right_rest = guarded(beside, left, right)
    (right_first,) = hold(right_first)
    base, weights = hold(base, weights)
    right_high, right_low = guarded(middle, right_first, right_rest)
    part = pl.pallas_call(
        own_kernel,
        out_shape=jax.ShapeDtypeStruct((4 * half, cols), f32),
        in_specs=[vmem] * 5,
        out_specs=vmem,
        compiler_params=PARAMS,
        cost_estimate=pl.CostEstimate(flops=3 << 26, bytes_accessed=2 << 20, transcendentals=0),
        name="own_layer",
    )(left_own, right_high, right_low, base, weights)
    own, core_out, chip_out, far_out = pl.pallas_call(
        mate_kernel,
        out_shape=(jax.ShapeDtypeStruct((half, cols), f32),) * 4,
        in_specs=[vmem] * 5,
        out_specs=(vmem,) * 4,
        compiler_params=PARAMS,
        cost_estimate=pl.CostEstimate(flops=3 << 26, bytes_accessed=2 << 20, transcendentals=0),
        name="mate_layer",
    )(left_mate, right_high, right_low, part, weights)
    chip_in = permute(chip_out, lambda l, r, c: (l ^ 2, r, c))
    far_in = permute(far_out, lambda l, r, c: (l ^ 3, r, c))
    core_in = permute(core_out, lambda l, r, c: (l ^ 1, r, c))
    chip_in, far_in = hold(chip_in, far_in)
    result = pl.pallas_call(
        last_kernel,
        out_shape=jax.ShapeDtypeStruct((rows, cols), f32),
        in_specs=[smem] + [vmem] * 4,
        out_specs=anywhere,
        scratch_shapes=[pltpu.VMEM((rows, cols), f32), pltpu.SemaphoreType.DMA((2,))],
        compiler_params=PARAMS,
        cost_estimate=pl.CostEstimate(flops=1 << 18, bytes_accessed=1 << 20, transcendentals=0),
        name="last_sum",
    )(keep_mask, chip_in, far_in, core_in, own)
    return result[None, None, None]


def solution(mesh):
    return jax.shard_map(
        local,
        mesh=mesh,
        in_specs=(
            P("layer", "row", "col", None, None, None),
            P("layer", "row", "col", None, None, None),
            P("layer", "row", "col", None, None),
            P("layer", "row", "col", None, None),
            P("layer", "row", "col", None, None),
            P("layer", "row", "col", None),
            P("row", "col", "layer"),
        ),
        out_specs=P("row", "col", "layer", None, None),
        check_vma=False,
    )
```
